32 devices in a mesh: groups: 2 (over y), node: 4 (over z), feat: 4 (over x, core).
Axes of the slice: x: 2, y: 2, z: 4, core: 2. Of those that a mesh axis runs over, the one named last changes fastest.
Arguments:
- features: bfloat16 [32768, 256], P(('groups', 'node'), 'feat'), parts along dimension 0, may hold values from -6 to 6
- weight: bfloat16 [256, 172], P('feat'), may hold values from -24 to 24
- block_cols: int32 [256, 8], P(('groups', 'node')), parts along dimension 0, may hold values from 0 to 127, as said below
- block_live: int32 [256, 8], P(('groups', 'node')), parts along dimension 0, may hold values 0 or 1
- block_tiles: bfloat16 [256, 8, 128, 128], P(('groups', 'node')), parts along dimension 0, may hold values from -0.1875 to 0.1875
- labels: int32 [32768], P(('groups', 'node')), parts along dimension 0, may hold values from 0 to 171
Outputs:
- loss: float32 [2], P('groups'), parts along dimension 0
- weight_grad: float32 [512, 172], P(('groups', 'feat')), parts along dimension 0
- grad_features: bfloat16 [32768, 256], P(('groups', 'node'), 'feat'), parts along dimension 0
The draws below stay inside these ranges and needn't reach their ends.
There are 2 independent parts, one for each index of `groups`. The reference program is written for one: setup_inputs(seed, part) draws one part's arguments, and reference() takes and returns one part's arrays. A program takes and returns all parts, laid end to end along the dimension named above; an argument that names none is the same for every part. Nothing has to cross between parts.
Inputs may be any that keep to these rules, and one draw needn't show every extreme that they name: `block_cols`: the 32 block rows of each index of node name, over their 8 slots, column blocks held at each index of node in exactly 64 slots.
All inputs are finite; a program needn't handle non-finite values. No bound on the sum of `block_live` on one device may be relied on, other than what follows from the above.
Results may differ from the reference program's by a relative error of at most 0.012.
The reference program's roundings to bfloat16 on the way (of `aggregated`, `grad_logits` and `grad_agg`) count: a program that leaves them out, or rounds other values in their place, can miss the bound.
Values may be sent and summed in bfloat16 or wider, within the bound.
A program may use at most 128 MiB of HBM per device.

```python
import math
from functools import partial
import jax
import jax.numpy as jnp
from jax import lax

HID = 256
CLS = 172
BLK = 128
KS = 8
NB_DEV = 32
BLOCKS = 128
NODES = 16384
N_NODE = 4


def draw_weight(key, part):
    key = jax.random.fold_in(key, 7)
    first_key, second_key = jax.random.split(key)
    values = jax.random.normal(first_key, (HID, CLS), jnp.float32) * HID ** (-0.5)
    column_scale = jnp.exp(jax.random.uniform(second_key, (1, CLS), jnp.float32, 0.0, math.log(3.0)))
    values = jnp.clip(values * column_scale, -24.0, 24.0)
    return values.astype(jnp.bfloat16)


def draw_block_cols(key, part):
    key = jax.random.fold_in(key, 11)
    order_key, first_key, second_key = jax.random.split(key, 3)
    slot_total = NB_DEV * KS
    device_keys = jax.random.split(order_key, N_NODE)
    orders = jax.vmap(lambda one_key: jax.random.permutation(one_key, slot_total))(device_keys)
    owners = (orders % N_NODE).astype(jnp.int32)
    first_pick = jax.random.randint(first_key, (N_NODE, slot_total), 0, NB_DEV, jnp.int32)
    second_pick = jax.random.randint(second_key, (N_NODE, slot_total), 0, NB_DEV, jnp.int32)
    local_block = jnp.minimum(first_pick, second_pick)
    columns = owners * NB_DEV + local_block
    return columns.reshape(N_NODE * NB_DEV, KS).astype(jnp.int32)


def touch_ends(array, rng, smallest, high):
    dims = array.shape
    place = [jax.random.randint(jax.random.fold_in(rng, axis), (), 0, dims[axis]) for axis in range(len(dims))]
    array = array.at[tuple(place)].set(smallest)
    longest = dims.index(max(dims))
    place[longest] = (place[longest] + 1) % dims[longest]
    return array.at[tuple(place)].set(high)


def block_levels(own_key, dims, shards, smallest, top_value):
    loudness = 1.0
    for dim, shards_of in shards:
        heights = jax.random.uniform(jax.random.fold_in(jax.random.fold_in(own_key, 6), dim), (shards_of,), jnp.float32, smallest / len(shards), top_value / len(shards))
        loudness = loudness * jnp.repeat(jnp.exp(heights), dims[dim] // shards_of).reshape((-1,) + (1,) * (len(dims) - 1 - dim))
    return loudness


def bell_draw(key, shape, deviation, bound, cuts=(), held_as=jnp.bfloat16):
    factor_of = block_levels(key, shape, cuts, -0.22, 0.18) if cuts else 1.0
    entries = jax.random.normal(key, shape, jnp.float32) * deviation * factor_of
    return jnp.minimum(jnp.maximum(entries, -bound), bound).astype(held_as)


def setup_inputs(seed: int = 0, part: int = 0) -> dict:
    key_list = jax.random.split(jax.random.key(seed), 7)
    own_keys = jax.random.split(jax.random.fold_in(key_list[6], part), 7)
    features = bell_draw(own_keys[0], (NODES, HID), 1.0, 6.0, ((0, 4), (1, 4)))
    weight = draw_weight(jax.random.fold_in(key_list[6], 71), part)
    block_cols = draw_block_cols(jax.random.fold_in(jax.random.fold_in(key_list[6], part), 71), part)
    block_live = touch_ends((jax.random.randint(own_keys[3], (BLOCKS, KS), 0, 4) < 3).astype(jnp.int32), jax.random.fold_in(own_keys[3], 1), 0, 1)
    block_tiles = bell_draw(own_keys[4], (BLOCKS, KS, BLK, BLK), (BLK * KS) ** -0.5, 0.1875, ((0, 4),))
    labels = touch_ends(jax.random.randint(own_keys[5], (NODES,), 0, CLS), jax.random.fold_in(own_keys[5], 1), 0, CLS - 1).astype(jnp.int32)
    return {"features": features, "weight": weight, "block_cols": block_cols, "block_live": block_live, "block_tiles": block_tiles, "labels": labels}


def softmax_terms(logits, labels):
    highest = jnp.max(logits, axis=1, keepdims=True)
    totals = jnp.sum(jnp.exp(logits - highest), axis=1, keepdims=True)
    logsum = highest + jnp.log(totals)
    onehot = labels[:, None] == jnp.arange(logits.shape[1], dtype=jnp.int32)[None, :]
    picked = jnp.sum(jnp.where(onehot, logits, 0.0), axis=1, keepdims=True)
    loss_sum = jnp.sum(logsum - picked).reshape(1)
    grad_logits = (jnp.exp(logits - logsum) - onehot.astype(logits.dtype)).astype(jnp.bfloat16)
    return loss_sum, grad_logits


def aggregate_row(blocks, inputs):
    tile_row, col_row, live_row = inputs
    panels = jnp.take(blocks, col_row, axis=0).astype(jnp.float32)
    panels = panels * live_row[:, None, None].astype(jnp.float32)
    return jnp.einsum('skm,smf->kf', tile_row.astype(jnp.float32), panels)


def spread_row(carried, inputs):
    tile_row, col_row, live_row, grad_row = inputs
    contrib = jnp.einsum('skm,kf->smf', tile_row.astype(jnp.float32), grad_row.astype(jnp.float32))
    contrib = contrib * live_row[:, None, None].astype(jnp.float32)
    return carried.at[col_row].add(contrib), None


def reference(features, weight, block_cols, block_live, block_tiles, labels):
    total_blocks = NB_DEV * N_NODE
    node_count = total_blocks * BLK
    blocks = features.reshape(total_blocks, BLK, HID)
    summed = lax.map(partial(aggregate_row, blocks), (block_tiles, block_cols, block_live))
    aggregated = summed.reshape(node_count, HID).astype(jnp.bfloat16)
    logits = jnp.dot(aggregated, weight, preferred_element_type=jnp.float32)
    loss_sum, grad_logits = softmax_terms(logits, labels)
    loss = loss_sum / node_count
    weight_grad = jnp.dot(aggregated.T, grad_logits, preferred_element_type=jnp.float32)
    grad_agg = jnp.dot(grad_logits, weight.T, preferred_element_type=jnp.float32).astype(jnp.bfloat16)
    grad_blocks = grad_agg.reshape(total_blocks, BLK, HID)
    start_sum = jnp.zeros((total_blocks, BLK, HID), jnp.float32)
    carried, _ = lax.scan(spread_row, start_sum, (block_tiles, block_cols, block_live, grad_blocks))
    grad_features = carried.reshape(node_count, HID).astype(jnp.bfloat16)
    return (loss, weight_grad, grad_features)
```

```python
import functools

import jax
import jax.numpy as jnp
from jax import lax
from jax.experimental import pallas as pl
from jax.experimental.pallas import tpu as pltpu
from jax.sharding import PartitionSpec as P

MESH = pl.DeviceIdType.MESH
NT = (((1,), (1,)), ((), ()))
UNROLL = 8


def kernel(dims, *refs):
    n, nf, classes, pad_classes, row_classes, slots = dims
    (x_ref, w_ref, lab_ref, tiles_hbm, order, lcol, rank, live, keep, last, has) = refs[:11]
    loss_ref, wg_ref, gf_ref = refs[11:14]
    rest = list(refs[14:])
    xown = rest.pop(0)
    xr = [rest.pop(0) for _ in range(n - 1)]
    xl = [rest.pop(0) for _ in range(n - 1)]
    (tiles, prod, agg, agr, gsend, gback, wfull, wgs, wgr, wz, wzs, wzr,
     sr, sl, rr, rl, tile_sem, xs_sem, xr_sem, ws_sem, wr_sem, as_sem, ar_sem,
     gs_sem, gr_sem, vs_sem, vr_sem, zs_sem, zr_sem, rs_sem, rv_sem) = rest

    blocks, feat, blk = xown.shape
    share = blocks // nf
    per = order.shape[0] // n
    z = lax.axis_index("node")
    f = lax.axis_index("feat")
    has_right, has_left = z < n - 1, z > 0

    def node_dev(i):
        return {"node": i}

    def feat_dev(i):
        return {"feat": i}

    def send(src, dst, s_sem, r_sem, device):
        return pltpu.make_async_remote_copy(
            src_ref=src, dst_ref=dst, send_sem=s_sem, recv_sem=r_sem,
            device_id=device, device_id_type=MESH)

    tile_copy = pltpu.make_async_copy(tiles_hbm, tiles, tile_sem)
    tile_copy.start()

    barrier = pltpu.get_barrier_semaphore()
    for d in range(1, nf):
        pl.semaphore_signal(barrier, inc=1, device_id=feat_dev(lax.rem(f + d, nf)), device_id_type=MESH)

    @pl.when(has_right)
    def _():
        pl.semaphore_signal(barrier, inc=1, device_id=node_dev(z + 1), device_id_type=MESH)

    @pl.when(has_left)
    def _():
        pl.semaphore_signal(barrier, inc=1, device_id=node_dev(z - 1), device_id_type=MESH)

    for b in range(blocks):
        xown[b] = x_ref[:, b * blk:(b + 1) * blk]
    wfull[f] = w_ref[...]
    pl.semaphore_wait(barrier, nf - 1 + has_right.astype(jnp.int32) + has_left.astype(jnp.int32))

    def x_right(s):
        return send(xown if s == 0 else xr[s - 1], xr[s], xs_sem.at[0, s], xr_sem.at[0, s], node_dev(z + 1))

    def x_left(s):
        return send(xown if s == 0 else xl[s - 1], xl[s], xs_sem.at[1, s], xr_sem.at[1, s], node_dev(z - 1))

    pl.when(has_right)(lambda: x_right(0).start())
    pl.when(has_left)(lambda: x_left(0).start())

    def w_copy(d):
        return send(wfull.at[f], wfull.at[f], ws_sem.at[d - 1], wr_sem.at[d - 1],
                    feat_dev(lax.rem(f + d, nf)))

    for d in range(1, nf):
        w_copy(d).start()

    tile_copy.wait()

    def forward_products(buf, owner):
        base = owner * per

        def body(step, carry):
            for u in range(UNROLL):
                t = base + step * UNROLL + u
                part = lax.dot_general(buf[lcol[t]], tiles[order[t]], NT,
                                       preferred_element_type=jnp.float32)
                prod[t] = part * live[t]
            return carry

        lax.fori_loop(0, per // UNROLL, body, 0)

    forward_products(xown, z)
    for s in range(n - 1):
        @pl.when(z - 1 - s >= 0)
        def _():
            x_right(s).wait_recv()
            if s + 1 < n - 1:
                pl.when(has_right)(lambda: x_right(s + 1).start())

        @pl.when(z + 1 + s < n)
        def _():
            x_left(s).wait_recv()
            if s + 1 < n - 1:
                pl.when(has_left)(lambda: x_left(s + 1).start())

        pl.when(z - 1 - s >= 0)(lambda: forward_products(xr[s], z - 1 - s))
        pl.when(z + 1 + s < n)(lambda: forward_products(xl[s], z + 1 + s))

    def a_copy(d):
        peer = lax.rem(f + d, nf)
        return send(agg.at[pl.ds(peer * share, share)], agr.at[f], as_sem.at[d - 1], ar_sem.at[d - 1],
                    feat_dev(peer))

    def sum_rows(first):
        def body(i, carry):
            row = first + i
            total = prod[rank[row * slots]]
            for s in range(1, slots):
                total = total + prod[rank[row * slots + s]]
            agg[row] = total.astype(jnp.bfloat16)
            return carry

        lax.fori_loop(0, share, body, 0)

    for d in list(range(nf - 1, 0, -1)):
        sum_rows(lax.rem(f + d, nf) * share)
        a_copy(d).start()
    sum_rows(f * share)
    agr[f] = agg[pl.ds(f * share, share)]

    for d in range(1, nf):
        w_copy(d).wait_recv()
    w_all = jnp.concatenate([wfull[i] for i in range(nf)], axis=0)
    w_turned = w_all.astype(jnp.float32).T.astype(jnp.bfloat16)[:row_classes]
    for d in range(1, nf):
        a_copy(d).wait_recv()

    class_row = lax.broadcasted_iota(jnp.int32, (row_classes, 2 * blk), 0)
    loss_row = jnp.zeros((1, 2 * blk), jnp.float32)
    wg = None
    for b in range(0, share, 2):
        part = jnp.concatenate(
            [jnp.concatenate([agr[i, b + c] for i in range(nf)], axis=0) for c in range(2)], axis=1)
        logits = jnp.dot(w_turned, part, preferred_element_type=jnp.float32)
        logits = jnp.where(class_row < classes, logits, -3e38)
        label = jnp.concatenate([lab_ref[pl.ds(f * share + b + c, 1), :] for c in range(2)], axis=1)
        onehot = class_row == label
        highest = jnp.max(logits, axis=0, keepdims=True)
        grown = jnp.exp(logits - highest)
        total = jnp.sum(grown, axis=0, keepdims=True)
        picked = jnp.sum(jnp.where(onehot, logits, 0.0), axis=0, keepdims=True)
        loss_row = loss_row + (highest + jnp.log(total) - picked)
        grad = grown * (1.0 / total) - jnp.where(onehot, 1.0, 0.0)
        grad = grad.astype(jnp.bfloat16)
        grad = jnp.concatenate(
            [grad, jnp.zeros((pad_classes - row_classes, 2 * blk), jnp.bfloat16)], axis=0)
        back = jnp.dot(w_all, grad, preferred_element_type=jnp.float32).astype(jnp.bfloat16)
        for i in range(nf):
            for c in range(2):
                gsend[i, b + c] = back[i * feat:(i + 1) * feat, c * blk:(c + 1) * blk]
        more = lax.dot_general(part, grad, NT, preferred_element_type=jnp.float32)
        wg = more if wg is None else wg + more

    def g_copy(d):
        peer = lax.rem(f + d, nf)
        return send(gsend.at[peer], gback.at[pl.ds(f * share, share)], gs_sem.at[d - 1], gr_sem.at[d - 1],
                    feat_dev(peer))

    def v_copy(d):
        peer = lax.rem(f + d, nf)
        return send(wgs.at[peer], wgr.at[d - 1], vs_sem.at[d - 1], vr_sem.at[d - 1], feat_dev(peer))

    for d in range(nf - 1, 0, -1):
        g_copy(d).start()
    for i in range(nf):
        wgs[i, :feat] = wg[i * feat:(i + 1) * feat]
        wgs[i, feat:] = jnp.broadcast_to(loss_row, (8, 2 * blk))
    for d in range(nf - 1, 0, -1):
        v_copy(d).start()
    gback[pl.ds(f * share, share)] = gsend[f]
    for d in range(1, nf):
        g_copy(d).wait_recv()

    def backward_products(owner):
        base = owner * per

        def body(step, total):
            for u in range(UNROLL):
                i = step * UNROLL + u
                t = base + i
                slot = order[t]
                part = jnp.dot(gback[lax.div(slot, slots)], tiles[slot],
                               preferred_element_type=jnp.float32)
                total = part * live[t] + total * keep[t]
                prod[i] = total
            return total

        lax.fori_loop(0, per // UNROLL, body, jnp.zeros((feat, blk), jnp.float32))

    def right_copy(k):
        return send(sr.at[k], rr.at[k], rs_sem.at[0, k], rv_sem.at[0, k], node_dev(z + 1))

    def left_copy(k):
        return send(sl.at[k], rl.at[k], rs_sem.at[1, k], rv_sem.at[1, k], node_dev(z - 1))

    def fill(out, came, owner):
        def body(j, carry):
            at = owner * blocks + j
            total = prod[last[at]] * has[at]
            if came is not None:
                total = total + came[j].astype(jnp.float32)
            out[j] = total.astype(jnp.bfloat16)
            return carry

        lax.fori_loop(0, blocks, body, 0)

    def z_right():
        return send(wzs.at[0], wzr.at[0], zs_sem.at[0], zr_sem.at[0], node_dev(z + 1))

    def z_left():
        return send(wzs.at[1], wzr.at[1], zs_sem.at[1], zr_sem.at[1], node_dev(z - 1))

    for k in range(n - 1):
        @pl.when(n - 1 - k > z)
        def _():
            owner = n - 1 - k
            backward_products(owner)

            @pl.when(has_left)
            def _():
                right_copy(k).wait_recv()
                fill(sr.at[k], rr.at[k], owner)

            pl.when(jnp.logical_not(has_left))(lambda: fill(sr.at[k], None, owner))
            right_copy(k).start()

        @pl.when(k < z)
        def _():
            backward_products(k)

            @pl.when(has_right)
            def _():
                left_copy(k).wait_recv()
                fill(sl.at[k], rl.at[k], k)

            pl.when(jnp.logical_not(has_right))(lambda: fill(sl.at[k], None, k))
            left_copy(k).start()

        if k == 0:
            own = wgs[f]
            for d in range(1, nf):
                v_copy(d).wait_recv()
                own = own + wgr[d - 1]
            wz[...] = own

            @pl.when(jnp.logical_not(has_left))
            def _():
                wzs[0] = wz[...]
                z_right().start()

            @pl.when(jnp.logical_not(has_right))
            def _():
                wzs[1] = wz[...]
                z_left().start()

        if k == min(1, n - 2):
            @pl.when(has_left)
            def _():
                z_right().wait_recv()

                @pl.when(has_right)
                def _():
                    wzs[0] = wz[...] + wzr[0]
                    z_right().start()

            @pl.when(has_right)
            def _():
                z_left().wait_recv()

                @pl.when(has_left)
                def _():
                    wzs[1] = wz[...] + wzr[1]
                    z_left().start()

    backward_products(z)

    pl.when(has_left)(lambda: right_copy(n - 1 - z).wait_recv())
    pl.when(has_right)(lambda: left_copy(z).wait_recv())
    one = jnp.where(has_left, 1.0, 0.0)
    two = jnp.where(has_right, 1.0, 0.0)

    @pl.when(jnp.logical_not(has_left))
    def _():
        rr[n - 1 - z] = jnp.zeros(rr.shape[1:], rr.dtype)
        wzr[0] = jnp.zeros(wzr.shape[1:], wzr.dtype)

    @pl.when(jnp.logical_not(has_right))
    def _():
        rl[z] = jnp.zeros(rl.shape[1:], rl.dtype)
        wzr[1] = jnp.zeros(wzr.shape[1:], wzr.dtype)

    for j in range(blocks):
        at = z * blocks + j
        total = prod[last[at]] * has[at]
        total = total + rr[n - 1 - z, j].astype(jnp.float32) + rl[z, j].astype(jnp.float32)
        gf_ref[:, j * blk:(j + 1) * blk] = total.astype(jnp.bfloat16)

    full = wz[...] + wzr[0] + wzr[1]
    wg_ref[...] = full[:feat, :classes]
    mean = jnp.sum(full[feat:feat + 1], axis=1, keepdims=True) / (n * blocks * blk)
    loss_ref[...] = jnp.broadcast_to(mean, loss_ref.shape)

    for s in range(n - 1):
        pl.when(jnp.logical_and(has_right, z - s >= 0))(lambda: x_right(s).wait_send())
        pl.when(jnp.logical_and(has_left, z + s < n))(lambda: x_left(s).wait_send())
        pl.when(n - 1 - s > z)(lambda: right_copy(s).wait_send())
        pl.when(s < z)(lambda: left_copy(s).wait_send())
    for d in range(1, nf):
        w_copy(d).wait_send()
        a_copy(d).wait_send()
        g_copy(d).wait_send()
        v_copy(d).wait_send()
    pl.when(has_right)(lambda: z_right().wait_send())
    pl.when(has_left)(lambda: z_left().wait_send())


def slot_lists(block_cols, block_live, n):
    blocks = block_cols.shape[0]
    cols = block_cols.reshape(-1)
    live = block_live.reshape(-1)
    count = cols.shape[0]
    spot = jnp.arange(count, dtype=jnp.int32)
    key = cols * count + spot
    rank = jnp.sum((key[None, :] < key[:, None]).astype(jnp.int32), axis=1)
    match = rank[None, :] == spot[:, None]
    order = jnp.sum(jnp.where(match, spot[None, :], 0), axis=1)
    sorted_cols = jnp.sum(jnp.where(match, cols[None, :], 0), axis=1)
    sorted_live = jnp.sum(jnp.where(match, live[None, :], 0), axis=1).astype(jnp.float32)
    lcol = lax.rem(sorted_cols, blocks)
    keep = jnp.concatenate([jnp.zeros((1,), jnp.bool_), sorted_cols[1:] == sorted_cols[:-1]])
    keep = keep.astype(jnp.float32)
    targets = jnp.arange(blocks * n, dtype=jnp.int32)
    upto = jnp.sum((cols[None, :] <= targets[:, None]).astype(jnp.int32), axis=1)
    has = jnp.any(cols[None, :] == targets[:, None], axis=1)
    last = jnp.where(has, lax.rem(upto - 1, count // n), 0)
    return order, lcol, rank, sorted_live, keep, last, has.astype(jnp.float32)


def local(features, weight, block_cols, block_live, block_tiles, labels):
    n, nf = lax.axis_size("node"), lax.axis_size("feat")
    rows, feat = features.shape
    blocks, slots, blk, _ = block_tiles.shape
    classes = weight.shape[1]
    pad_classes = 256 * pl.cdiv(classes, 256)
    row_classes = 16 * pl.cdiv(classes, 16)
    share = blocks // nf
    lists = slot_lists(block_cols, block_live, n)
    wide = jnp.pad(weight, ((0, 0), (0, pad_classes - classes)))
    bf, f32 = jnp.bfloat16, jnp.float32
    vmem = pl.BlockSpec(memory_space=pltpu.VMEM)
    smem = pl.BlockSpec(memory_space=pltpu.SMEM)
    panel = (blocks, feat, blk)
    dma = pltpu.SemaphoreType.DMA
    scratch = [pltpu.VMEM(panel, bf) for _ in range(2 * n - 1)] + [
        pltpu.VMEM((blocks * slots, blk, blk), bf),
        pltpu.VMEM((blocks * slots, feat, blk), f32),
        pltpu.VMEM(panel, bf),
        pltpu.VMEM((nf, share, feat, blk), bf),
        pltpu.VMEM((nf, share, feat, blk), bf),
        pltpu.VMEM(panel, bf),
        pltpu.VMEM((nf, feat, pad_classes), bf),
        pltpu.VMEM((nf, feat + 8, pad_classes), f32),
        pltpu.VMEM((nf - 1, feat + 8, pad_classes), f32),
        pltpu.VMEM((feat + 8, pad_classes), f32),
        pltpu.VMEM((2, feat + 8, pad_classes), f32),
        pltpu.VMEM((2, feat + 8, pad_classes), f32),
        pltpu.VMEM((n - 1,) + panel, bf),
        pltpu.VMEM((n - 1,) + panel, bf),
        pltpu.VMEM((n,) + panel, bf),
        pltpu.VMEM((n,) + panel, bf),
        dma, dma((2, n - 1)), dma((2, n - 1)),
        dma((nf - 1,)), dma((nf - 1,)), dma((nf - 1,)), dma((nf - 1,)),
        dma((nf - 1,)), dma((nf - 1,)), dma((nf - 1,)), dma((nf - 1,)),
        dma((2,)), dma((2,)), dma((2, n)), dma((2, n)),
    ]
    loss, weight_grad, turned = pl.pallas_call(
        functools.partial(kernel, (n, nf, classes, pad_classes, row_classes, slots)),
        out_shape=(
            jax.ShapeDtypeStruct((8, 128), f32),
            jax.ShapeDtypeStruct((feat, classes), f32),
            jax.ShapeDtypeStruct((feat, rows), bf),
        ),
        in_specs=[vmem, vmem, vmem, pl.BlockSpec(memory_space=pl.ANY)] + [smem] * 7,
        out_specs=(vmem, vmem, vmem),
        scratch_shapes=scratch,
        compiler_params=pltpu.CompilerParams(
            collective_id=0, has_side_effects=True, vmem_limit_bytes=56 * 1024 * 1024),
    )(features.T, wide, labels.reshape(blocks, blk),
      block_tiles.reshape(blocks * slots, blk, blk), *lists)
    return loss[0, :1], weight_grad, turned.T


def solution(mesh):
    placed = (
        P(("groups", "node"), "feat"),
        P("feat", None),
        P(("groups", "node"), None),
        P(("groups", "node"), None),
        P(("groups", "node"), None, None, None),
        P(("groups", "node")),
    )
    return jax.shard_map(
        local,
        mesh=mesh,
        in_specs=placed,
        out_specs=(P("groups"), P(("groups", "feat"), None), P(("groups", "node"), "feat")),
        check_vma=False,
    )
```

```python
import functools

import jax
import jax.numpy as jnp
from jax import lax
from jax.experimental import pallas as pl
from jax.experimental.pallas import tpu as pltpu
from jax.sharding import PartitionSpec as P

MESH = pl.DeviceIdType.MESH
NT = (((1,), (1,)), ((), ()))
UNROLL = 8


def kernel(dims, *refs):
    n, nf, classes, pad_classes, row_classes, slots = dims
    (x_ref, w_ref, lab_ref, slot_ref, tiles_hbm) = refs[:5]
    loss_ref, wg_ref, gf_ref = refs[5:8]
    rest = list(refs[8:])
    xown = rest.pop(0)
    xr = [rest.pop(0) for _ in range(n - 1)]
    xl = [rest.pop(0) for _ in range(n - 1)]
    (tiles, prod, agg, agr, gsend, gback, wfull, wgs, wgr, wz, wzs, wzr,
     sr, sl, rr, rl, tile_sem, xs_sem, xr_sem, ws_sem, wr_sem, as_sem, ar_sem,
     gs_sem, gr_sem, vs_sem, vr_sem, zs_sem, zr_sem, rs_sem, rv_sem,
     found, ends, lists, tops, list_sem) = rest

    blocks, feat, blk = xown.shape
    share = blocks // nf
    per = blocks * slots // n
    z = lax.axis_index("node")
    f = lax.axis_index("feat")
    has_right, has_left = z < n - 1, z > 0

    def node_dev(i):
        return {"node": i}

    def feat_dev(i):
        return {"feat": i}

    def send(src, dst, s_sem, r_sem, device):
        return pltpu.make_async_remote_copy(
            src_ref=src, dst_ref=dst, send_sem=s_sem, recv_sem=r_sem,
            device_id=device, device_id_type=MESH)

    tile_copy = pltpu.make_async_copy(tiles_hbm, tiles, tile_sem)
    tile_copy.start()

    barrier = pltpu.get_barrier_semaphore()
    for d in range(1, nf):
        pl.semaphore_signal(barrier, inc=1, device_id=feat_dev(lax.rem(f + d, nf)), device_id_type=MESH)

    @pl.when(has_right)
    def _():
        pl.semaphore_signal(barrier, inc=1, device_id=node_dev(z + 1), device_id_type=MESH)

    @pl.when(has_left)
    def _():
        pl.semaphore_signal(barrier, inc=1, device_id=node_dev(z - 1), device_id_type=MESH)

    for b in range(blocks):
        xown[b] = x_ref[:, b * blk:(b + 1) * blk]
    wfull[f] = jnp.concatenate(
        [w_ref[...], jnp.zeros((feat, pad_classes - classes), jnp.bfloat16)], axis=1)
    pl.semaphore_wait(barrier, nf - 1 + has_right.astype(jnp.int32) + has_left.astype(jnp.int32))

    def x_right(s):
        return send(xown if s == 0 else xr[s - 1], xr[s], xs_sem.at[0, s], xr_sem.at[0, s], node_dev(z + 1))

    def x_left(s):
        return send(xown if s == 0 else xl[s - 1], xl[s], xs_sem.at[1, s], xr_sem.at[1, s], node_dev(z - 1))

    pl.when(has_right)(lambda: x_right(0).start())
    pl.when(has_left)(lambda: x_left(0).start())

    def w_copy(d):
        return send(wfull.at[f], wfull.at[f], ws_sem.at[d - 1], wr_sem.at[d - 1],
                    feat_dev(lax.rem(f + d, nf)))

    for d in range(1, nf):
        w_copy(d).start()

    found[...], ends[...] = slot_lists(slot_ref[...], blocks, n)
    list_copy = pltpu.make_async_copy(found, lists, list_sem.at[0])
    top_copy = pltpu.make_async_copy(ends, tops, list_sem.at[1])
    list_copy.start()
    top_copy.start()
    list_copy.wait()
    top_copy.wait()

    tile_copy.wait()

    def forward_products(buf, owner):
        base = owner * per

        def body(step, carry):
            for u in range(UNROLL):
                t = base + step * UNROLL + u
                part = lax.dot_general(buf[lists[1, t]], tiles[lists[0, t]], NT,
                                       preferred_element_type=jnp.float32)
                prod[t] = part * lists[3, t].astype(jnp.float32)
            return carry

        lax.fori_loop(0, per // UNROLL, body, 0)

    forward_products(xown, z)
    for s in range(n - 1):
        @pl.when(z - 1 - s >= 0)
        def _():
            x_right(s).wait_recv()
            if s + 1 < n - 1:
                pl.when(has_right)(lambda: x_right(s + 1).start())

        @pl.when(z + 1 + s < n)
        def _():
            x_left(s).wait_recv()
            if s + 1 < n - 1:
                pl.when(has_left)(lambda: x_left(s + 1).start())

        pl.when(z - 1 - s >= 0)(lambda: forward_products(xr[s], z - 1 - s))
        pl.when(z + 1 + s < n)(lambda: forward_products(xl[s], z + 1 + s))

    def a_copy(d):
        peer = lax.rem(f + d, nf)
        return send(agg.at[pl.ds(peer * share, share)], agr.at[f], as_sem.at[d - 1], ar_sem.at[d - 1],
                    feat_dev(peer))

    def sum_rows(first):
        def body(i, carry):
            row = first + i
            total = prod[lists[2, row * slots]]
            for s in range(1, slots):
                total = total + prod[lists[2, row * slots + s]]
            agg[row] = total.astype(jnp.bfloat16)
            return carry

        lax.fori_loop(0, share, body, 0)

    for d in list(range(nf - 1, 0, -1)):
        sum_rows(lax.rem(f + d, nf) * share)
        a_copy(d).start()
    sum_rows(f * share)
    agr[f] = agg[pl.ds(f * share, share)]

    for d in range(1, nf):
        w_copy(d).wait_recv()
    w_all = jnp.concatenate([wfull[i] for i in range(nf)], axis=0)
    w_turned = w_all.astype(jnp.float32).T.astype(jnp.bfloat16)[:row_classes]
    for d in range(1, nf):
        a_copy(d).wait_recv()

    class_row = lax.broadcasted_iota(jnp.int32, (row_classes, 2 * blk), 0)
    loss_row = jnp.zeros((1, 2 * blk), jnp.float32)
    wg = None
    for b in range(0, share, 2):
        part = jnp.concatenate(
            [jnp.concatenate([agr[i, b + c] for i in range(nf)], axis=0) for c in range(2)], axis=1)
        logits = jnp.dot(w_turned, part, preferred_element_type=jnp.float32)
        logits = jnp.where(class_row < classes, logits, -3e38)
        label = jnp.concatenate([lab_ref[pl.ds(f * share + b + c, 1), :] for c in range(2)], axis=1)
        onehot = class_row == label
        highest = jnp.max(logits, axis=0, keepdims=True)
        grown = jnp.exp(logits - highest)
        total = jnp.sum(grown, axis=0, keepdims=True)
        picked = jnp.sum(jnp.where(onehot, logits, 0.0), axis=0, keepdims=True)
        loss_row = loss_row + (highest + jnp.log(total) - picked)
        grad = grown * (1.0 / total) - jnp.where(onehot, 1.0, 0.0)
        grad = grad.astype(jnp.bfloat16)
        grad = jnp.concatenate(
            [grad, jnp.zeros((pad_classes - row_classes, 2 * blk), jnp.bfloat16)], axis=0)
        back = jnp.dot(w_all, grad, preferred_element_type=jnp.float32).astype(jnp.bfloat16)
        for i in range(nf):
            for c in range(2):
                gsend[i, b + c] = back[i * feat:(i + 1) * feat, c * blk:(c + 1) * blk]
        more = lax.dot_general(part, grad, NT, preferred_element_type=jnp.float32)
        wg = more if wg is None else wg + more

    def g_copy(d):
        peer = lax.rem(f + d, nf)
        return send(gsend.at[peer], gback.at[pl.ds(f * share, share)], gs_sem.at[d - 1], gr_sem.at[d - 1],
                    feat_dev(peer))

    def v_copy(d):
        peer = lax.rem(f + d, nf)
        return send(wgs.at[peer], wgr.at[d - 1], vs_sem.at[d - 1], vr_sem.at[d - 1], feat_dev(peer))

    for d in range(nf - 1, 0, -1):
        g_copy(d).start()
    for i in range(nf):
        wgs[i, :feat] = wg[i * feat:(i + 1) * feat]
        wgs[i, feat:] = jnp.broadcast_to(loss_row, (8, 2 * blk))
    for d in range(nf - 1, 0, -1):
        v_copy(d).start()
    gback[pl.ds(f * share, share)] = gsend[f]
    for d in range(1, nf):
        g_copy(d).wait_recv()

    def backward_products(owner):
        base = owner * per

        def body(step, total):
            for u in range(UNROLL):
                i = step * UNROLL + u
                t = base + i
                slot = lists[0, t]
                part = jnp.dot(gback[lax.div(slot, slots)], tiles[slot],
                               preferred_element_type=jnp.float32)
                total = part * lists[3, t].astype(jnp.float32) + total * lists[4, t].astype(jnp.float32)
                prod[i] = total
            return total

        lax.fori_loop(0, per // UNROLL, body, jnp.zeros((feat, blk), jnp.float32))

    def right_copy(k):
        return send(sr.at[k], rr.at[k], rs_sem.at[0, k], rv_sem.at[0, k], node_dev(z + 1))

    def left_copy(k):
        return send(sl.at[k], rl.at[k], rs_sem.at[1, k], rv_sem.at[1, k], node_dev(z - 1))

    def fill(out, came, owner):
        def body(j, carry):
            at = owner * blocks + j
            total = prod[tops[0, at]] * tops[1, at].astype(jnp.float32)
            if came is not None:
                total = total + came[j].astype(jnp.float32)
            out[j] = total.astype(jnp.bfloat16)
            return carry

        lax.fori_loop(0, blocks, body, 0)

    def z_right():
        return send(wzs.at[0], wzr.at[0], zs_sem.at[0], zr_sem.at[0], node_dev(z + 1))

    def z_left():
        return send(wzs.at[1], wzr.at[1], zs_sem.at[1], zr_sem.at[1], node_dev(z - 1))

    for tick in range(n - 1):
        kr = tick - z
        kl = tick - (n - 1 - z)

        @pl.when(kr >= 0)
        def _():
            owner = n - 1 - kr
            backward_products(owner)

            @pl.when(has_left)
            def _():
                right_copy(kr).wait_recv()
                fill(sr.at[kr], rr.at[kr], owner)

            pl.when(jnp.logical_not(has_left))(lambda: fill(sr.at[kr], None, owner))
            right_copy(kr).start()

        @pl.when(kl >= 0)
        def _():
            backward_products(kl)

            @pl.when(has_right)
            def _():
                left_copy(kl).wait_recv()
                fill(sl.at[kl], rl.at[kl], kl)

            pl.when(jnp.logical_not(has_right))(lambda: fill(sl.at[kl], None, kl))
            left_copy(kl).start()

        if tick == 0:
            own = wgs[f]
            for d in range(1, nf):
                v_copy(d).wait_recv()
                own = own + wgr[d - 1]
            wz[...] = own

            @pl.when(jnp.logical_not(has_left))
            def _():
                wzs[0] = wz[...]
                z_right().start()

            @pl.when(jnp.logical_not(has_right))
            def _():
                wzs[1] = wz[...]
                z_left().start()

            @pl.when(jnp.logical_and(has_left, has_right))
            def _():
                z_right().wait_recv()
                wzs[0] = wz[...] + wzr[0]
                z_right().start()
                z_left().wait_recv()
                wzs[1] = wz[...] + wzr[1]
                z_left().start()

    backward_products(z)

    pl.when(has_left)(lambda: right_copy(n - 1 - z).wait_recv())
    pl.when(has_right)(lambda: left_copy(z).wait_recv())
    pl.when(jnp.logical_not(has_right))(lambda: z_right().wait_recv())
    pl.when(jnp.logical_not(has_left))(lambda: z_left().wait_recv())

    @pl.when(jnp.logical_not(has_left))
    def _():
        rr[n - 1 - z] = jnp.zeros(rr.shape[1:], rr.dtype)
        wzr[0] = jnp.zeros(wzr.shape[1:], wzr.dtype)

    @pl.when(jnp.logical_not(has_right))
    def _():
        rl[z] = jnp.zeros(rl.shape[1:], rl.dtype)
        wzr[1] = jnp.zeros(wzr.shape[1:], wzr.dtype)

    for j in range(blocks):
        at = z * blocks + j
        total = prod[tops[0, at]] * tops[1, at].astype(jnp.float32)
        total = total + rr[n - 1 - z, j].astype(jnp.float32) + rl[z, j].astype(jnp.float32)
        gf_ref[:, j * blk:(j + 1) * blk] = total.astype(jnp.bfloat16)

    full = wz[...] + wzr[0] + wzr[1]
    wg_ref[...] = full[:feat, :classes]
    mean = jnp.sum(full[feat:feat + 1], axis=1, keepdims=True) / (n * blocks * blk)
    loss_ref[...] = jnp.broadcast_to(mean, loss_ref.shape)

    for s in range(n - 1):
        pl.when(jnp.logical_and(has_right, z - s >= 0))(lambda: x_right(s).wait_send())
        pl.when(jnp.logical_and(has_left, z + s < n))(lambda: x_left(s).wait_send())
        pl.when(n - 1 - s > z)(lambda: right_copy(s).wait_send())
        pl.when(s < z)(lambda: left_copy(s).wait_send())
    for d in range(1, nf):
        w_copy(d).wait_send()
        a_copy(d).wait_send()
        g_copy(d).wait_send()
        v_copy(d).wait_send()
    pl.when(has_right)(lambda: z_right().wait_send())
    pl.when(has_left)(lambda: z_left().wait_send())


def slot_lists(packed, blocks, n):
    count = packed.shape[1]
    down = lax.broadcasted_iota(jnp.int32, (count, count), 0)
    across = lax.broadcasted_iota(jnp.int32, (count, count), 1)

    def upright(row):
        return jnp.sum(jnp.where(down == across, row, 0), axis=1, keepdims=True)

    cols, live = lax.shift_right_logical(packed, 1), packed & 1
    key = cols * count + across[:1]
    key_up, cols_up, live_up = upright(key), upright(cols), upright(live)
    rank = jnp.sum((key_up < key).astype(jnp.int32), axis=0, keepdims=True)
    match = upright(rank) == across

    def in_order(values_up):
        return jnp.sum(jnp.where(match, values_up, 0), axis=0, keepdims=True)

    order, sorted_cols = in_order(down), in_order(cols_up)
    sorted_up = upright(sorted_cols)
    before = jnp.sum(jnp.where(down + 1 == across, sorted_up, 0), axis=0, keepdims=True)
    keep = jnp.where(across[:1] > 0, (before == sorted_cols).astype(jnp.int32), 0)
    lcol = sorted_cols % blocks
    found = jnp.concatenate([order, lcol, rank, in_order(live_up), keep, keep, keep, keep], axis=0)
    target = lax.broadcasted_iota(jnp.int32, (count, blocks * n), 1)
    upto = jnp.sum((cols_up <= target).astype(jnp.int32), axis=0, keepdims=True)
    has = jnp.max((cols_up == target).astype(jnp.int32), axis=0, keepdims=True)
    last = jnp.where(has > 0, (upto - 1) % (count // n), 0)
    ends = jnp.concatenate([last, has, has, has, has, has, has, has], axis=0)
    return found, ends


def local(features, weight, block_cols, block_live, block_tiles, labels):
    n, nf = lax.axis_size("node"), lax.axis_size("feat")
    rows, feat = features.shape
    blocks, slots, blk, _ = block_tiles.shape
    classes = weight.shape[1]
    pad_classes = 256 * pl.cdiv(classes, 256)
    row_classes = 16 * pl.cdiv(classes, 16)
    share = blocks // nf
    packed = (block_cols * 2 + block_live).reshape(1, blocks * slots)
    i32 = jnp.int32
    count = blocks * slots
    bf, f32 = jnp.bfloat16, jnp.float32
    vmem = pl.BlockSpec(memory_space=pltpu.VMEM)
    panel = (blocks, feat, blk)
    dma = pltpu.SemaphoreType.DMA
    scratch = [pltpu.VMEM(panel, bf) for _ in range(2 * n - 1)] + [
        pltpu.VMEM((blocks * slots, blk, blk), bf),
        pltpu.VMEM((blocks * slots, feat, blk), f32),
        pltpu.VMEM(panel, bf),
        pltpu.VMEM((nf, share, feat, blk), bf),
        pltpu.VMEM((nf, share, feat, blk), bf),
        pltpu.VMEM(panel, bf),
        pltpu.VMEM((nf, feat, pad_classes), bf),
        pltpu.VMEM((nf, feat + 8, pad_classes), f32),
        pltpu.VMEM((nf - 1, feat + 8, pad_classes), f32),
        pltpu.VMEM((feat + 8, pad_classes), f32),
        pltpu.VMEM((2, feat + 8, pad_classes), f32),
        pltpu.VMEM((2, feat + 8, pad_classes), f32),
        pltpu.VMEM((n - 1,) + panel, bf),
        pltpu.VMEM((n - 1,) + panel, bf),
        pltpu.VMEM((n,) + panel, bf),
        pltpu.VMEM((n,) + panel, bf),
        dma, dma((2, n - 1)), dma((2, n - 1)),
        dma((nf - 1,)), dma((nf - 1,)), dma((nf - 1,)), dma((nf - 1,)),
        dma((nf - 1,)), dma((nf - 1,)), dma((nf - 1,)), dma((nf - 1,)),
        dma((2,)), dma((2,)), dma((2, n)), dma((2, n)),
        pltpu.VMEM((8, count), i32), pltpu.VMEM((8, blocks * n), i32),
        pltpu.SMEM((8, count), i32), pltpu.SMEM((8, blocks * n), i32), dma((2,)),
    ]
    loss, weight_grad, turned = pl.pallas_call(
        functools.partial(kernel, (n, nf, classes, pad_classes, row_classes, slots)),
        out_shape=(
            jax.ShapeDtypeStruct((8, 128), f32),
            jax.ShapeDtypeStruct((feat, classes), f32),
            jax.ShapeDtypeStruct((feat, rows), bf),
        ),
        in_specs=[vmem, vmem, vmem, vmem, pl.BlockSpec(memory_space=pl.ANY)],
        out_specs=(vmem, vmem, vmem),
        scratch_shapes=scratch,
        compiler_params=pltpu.CompilerParams(
            collective_id=0, has_side_effects=True, vmem_limit_bytes=56 * 1024 * 1024),
    )(features.T, weight, labels.reshape(blocks, blk), packed,
      block_tiles.reshape(blocks * slots, blk, blk))
    return loss[0, :1], weight_grad, turned.T


def solution(mesh):
    placed = (
        P(("groups", "node"), "feat"),
        P("feat", None),
        P(("groups", "node"), None),
        P(("groups", "node"), None),
        P(("groups", "node"), None, None, None),
        P(("groups", "node")),
    )
    return jax.shard_map(
        local,
        mesh=mesh,
        in_specs=placed,
        out_specs=(P("groups"), P(("groups", "feat"), None), P(("groups", "node"), "feat")),
        check_vma=False,
    )
```

```python
import functools

import jax
import jax.numpy as jnp
from jax import lax
from jax.experimental import pallas as pl
from jax.experimental.pallas import tpu as pltpu
from jax.sharding import PartitionSpec as P

MESH = pl.DeviceIdType.MESH
NT = (((1,), (1,)), ((), ()))
UNROLL = 16
HALVES = 2


def kernel(dims, *refs):
    n, nf, classes, pad_classes, row_classes, slots = dims
    (x_ref, w_ref, lab_ref, slot_ref, tiles_hbm) = refs[:5]
    loss_ref, wg_ref, gf_ref = refs[5:8]
    rest = list(refs[8:])
    xown = rest.pop(0)
    xr = [rest.pop(0) for _ in range(n - 1)]
    xl = [rest.pop(0) for _ in range(n - 1)]
    (tiles, prod, agg, agr, gsend, gback, wfull, wgs, wgr, wz, wzs, wzr,
     sr, sl, rr, rl, tile_sem, xs_sem, xr_sem, ws_sem, wr_sem, as_sem, ar_sem,
     gs_sem, gr_sem, vs_sem, vr_sem, zs_sem, zr_sem, rs_sem, rv_sem,
     found, ends, lists, tops, list_sem) = rest

    blocks, feat, blk = xown.shape
    share = blocks // nf
    per = blocks * slots // n
    unroll = min(UNROLL, per)
    half = blocks // HALVES
    z = lax.axis_index("node")
    f = lax.axis_index("feat")
    has_right, has_left = z < n - 1, z > 0

    def node_dev(i):
        return {"node": i}

    def feat_dev(i):
        return {"feat": i}

    def send(src, dst, s_sem, r_sem, device):
        return pltpu.make_async_remote_copy(
            src_ref=src, dst_ref=dst, send_sem=s_sem, recv_sem=r_sem,
            device_id=device, device_id_type=MESH)

    tile_copy = pltpu.make_async_copy(tiles_hbm, tiles, tile_sem)
    tile_copy.start()

    barrier = pltpu.get_barrier_semaphore()
    for d in range(1, nf):
        pl.semaphore_signal(barrier, inc=1, device_id=feat_dev(lax.rem(f + d, nf)), device_id_type=MESH)

    @pl.when(has_right)
    def _():
        pl.semaphore_signal(barrier, inc=1, device_id=node_dev(z + 1), device_id_type=MESH)

    @pl.when(has_left)
    def _():
        pl.semaphore_signal(barrier, inc=1, device_id=node_dev(z - 1), device_id_type=MESH)

    for b in range(blocks):
        xown[b] = x_ref[:, b * blk:(b + 1) * blk]
    wfull[f] = jnp.concatenate(
        [w_ref[...], jnp.zeros((feat, pad_classes - classes), jnp.bfloat16)], axis=1)
    pl.semaphore_wait(barrier, nf - 1 + has_right.astype(jnp.int32) + has_left.astype(jnp.int32))

    def part(ref, h):
        return ref.at[pl.ds(h * half, half)]

    def x_right(s, h):
        return send(part(xown if s == 0 else xr[s - 1], h), part(xr[s], h),
                    xs_sem.at[0, s, h], xr_sem.at[0, s, h], node_dev(z + 1))

    def x_left(s, h):
        return send(part(xown if s == 0 else xl[s - 1], h), part(xl[s], h),
                    xs_sem.at[1, s, h], xr_sem.at[1, s, h], node_dev(z - 1))

    for h in range(HALVES):
        pl.when(has_right)(lambda: x_right(0, h).start())
        pl.when(has_left)(lambda: x_left(0, h).start())

    def w_copy(d):
        return send(wfull.at[f], wfull.at[f], ws_sem.at[d - 1], wr_sem.at[d - 1],
                    feat_dev(lax.rem(f + d, nf)))

    for d in range(1, nf):
        w_copy(d).start()

    found[...], ends[...] = slot_lists(slot_ref[...], blocks, n)
    list_copy = pltpu.make_async_copy(found, lists, list_sem.at[0])
    top_copy = pltpu.make_async_copy(ends, tops, list_sem.at[1])
    list_copy.start()
    top_copy.start()
    list_copy.wait()
    top_copy.wait()

    tile_copy.wait()

    def forward_products(buf, owner):
        base = owner * per

        def body(step, carry):
            for u in range(unroll):
                t = base + step * unroll + u
                product = lax.dot_general(buf[lists[1, t]], tiles[lists[0, t]], NT,
                                       preferred_element_type=jnp.float32)
                prod[t] = product * lists[3, t].astype(jnp.float32)
            return carry

        lax.fori_loop(0, per // unroll, body, 0)

    forward_products(xown, z)
    for s in range(n - 1):
        for h in range(HALVES):
            @pl.when(z - 1 - s >= 0)
            def _():
                x_right(s, h).wait_recv()
                if s + 1 < n - 1:
                    pl.when(has_right)(lambda: x_right(s + 1, h).start())

            @pl.when(z + 1 + s < n)
            def _():
                x_left(s, h).wait_recv()
                if s + 1 < n - 1:
                    pl.when(has_left)(lambda: x_left(s + 1, h).start())

        pl.when(z - 1 - s >= 0)(lambda: forward_products(xr[s], z - 1 - s))
        pl.when(z + 1 + s < n)(lambda: forward_products(xl[s], z + 1 + s))

    def a_copy(d):
        peer = lax.rem(f + d, nf)
        return send(agg.at[pl.ds(peer * share, share)], agr.at[f], as_sem.at[d - 1], ar_sem.at[d - 1],
                    feat_dev(peer))

    def sum_rows(first):
        def body(i, carry):
            row = first + i
            total = prod[lists[2, row * slots]]
            for s in range(1, slots):
                total = total + prod[lists[2, row * slots + s]]
            agg[row] = total.astype(jnp.bfloat16)
            return carry

        lax.fori_loop(0, share, body, 0)

    far_first = sorted(range(1, nf), key=lambda d: abs(d - nf // 2))
    for d in far_first:
        sum_rows(lax.rem(f + d, nf) * share)
        a_copy(d).start()
    sum_rows(f * share)
    agr[f] = agg[pl.ds(f * share, share)]

    for d in range(1, nf):
        w_copy(d).wait_recv()
    w_all = jnp.concatenate([wfull[i] for i in range(nf)], axis=0)
    w_turned = w_all.astype(jnp.float32).T.astype(jnp.bfloat16)[:row_classes]
    for d in range(1, nf):
        a_copy(d).wait_recv()

    class_row = lax.broadcasted_iota(jnp.int32, (row_classes, 2 * blk), 0)
    loss_row = jnp.zeros((1, 2 * blk), jnp.float32)
    wg = None
    for b in range(0, share, 2):
        whole = jnp.concatenate(
            [jnp.concatenate([agr[i, b + c] for i in range(nf)], axis=0) for c in range(2)], axis=1)
        logits = jnp.dot(w_turned, whole, preferred_element_type=jnp.float32)
        logits = jnp.where(class_row < classes, logits, -3e38)
        label = jnp.concatenate([lab_ref[pl.ds(f * share + b + c, 1), :] for c in range(2)], axis=1)
        onehot = class_row == label
        highest = jnp.max(logits, axis=0, keepdims=True)
        grown = jnp.exp(logits - highest)
        total = jnp.sum(grown, axis=0, keepdims=True)
        picked = jnp.sum(jnp.where(onehot, logits, 0.0), axis=0, keepdims=True)
        loss_row = loss_row + (highest + jnp.log(total) - picked)
        grad = grown * (1.0 / total) - jnp.where(onehot, 1.0, 0.0)
        grad = grad.astype(jnp.bfloat16)
        grad = jnp.concatenate(
            [grad, jnp.zeros((pad_classes - row_classes, 2 * blk), jnp.bfloat16)], axis=0)
        back = jnp.dot(w_all, grad, preferred_element_type=jnp.float32).astype(jnp.bfloat16)
        for i in range(nf):
            for c in range(2):
                gsend[i, b + c] = back[i * feat:(i + 1) * feat, c * blk:(c + 1) * blk]
        more = lax.dot_general(whole, grad, NT, preferred_element_type=jnp.float32)
        wg = more if wg is None else wg + more

    def g_copy(d):
        peer = lax.rem(f + d, nf)
        return send(gsend.at[peer], gback.at[pl.ds(f * share, share)], gs_sem.at[d - 1], gr_sem.at[d - 1],
                    feat_dev(peer))

    def v_copy(d):
        peer = lax.rem(f + d, nf)
        return send(wgs.at[peer], wgr.at[d - 1], vs_sem.at[d - 1], vr_sem.at[d - 1], feat_dev(peer))

    for d in far_first:
        g_copy(d).start()
    for i in range(nf):
        wgs[i, :feat] = wg[i * feat:(i + 1) * feat]
        wgs[i, feat:] = jnp.broadcast_to(loss_row, (8, 2 * blk))
    for d in far_first:
        v_copy(d).start()
    gback[pl.ds(f * share, share)] = gsend[f]
    for d in range(1, nf):
        g_copy(d).wait_recv()

    def backward_products(owner):
        base = owner * per

        def body(step, total):
            for u in range(unroll):
                i = step * unroll + u
                t = base + i
                slot = lists[0, t]
                product = jnp.dot(gback[lax.div(slot, slots)], tiles[slot],
                               preferred_element_type=jnp.float32)
                total = product * lists[3, t].astype(jnp.float32) + total * lists[4, t].astype(jnp.float32)
                prod[i] = total
            return total

        lax.fori_loop(0, per // unroll, body, jnp.zeros((feat, blk), jnp.float32))

    def right_copy(k, h):
        return send(part(sr.at[k], h), part(rr.at[k], h), rs_sem.at[0, k, h], rv_sem.at[0, k, h], node_dev(z + 1))

    def left_copy(k, h):
        return send(part(sl.at[k], h), part(rl.at[k], h), rs_sem.at[1, k, h], rv_sem.at[1, k, h], node_dev(z - 1))

    def fill(out, came, owner, h):
        def body(j, carry):
            at = owner * blocks + j
            total = prod[tops[0, at]] * tops[1, at].astype(jnp.float32)
            if came is not None:
                total = total + came[j].astype(jnp.float32)
            out[j] = total.astype(jnp.bfloat16)
            return carry

        lax.fori_loop(h * half, (h + 1) * half, body, 0)

    def pass_on(copy, k, out, came, owner, inside):
        for h in range(HALVES):
            @pl.when(inside)
            def _():
                copy(k, h).wait_recv()
                fill(out.at[k], came.at[k], owner, h)

            pl.when(jnp.logical_not(inside))(lambda: fill(out.at[k], None, owner, h))
            copy(k, h).start()

    def z_right():
        return send(wzs.at[0], wzr.at[0], zs_sem.at[0], zr_sem.at[0], node_dev(z + 1))

    def z_left():
        return send(wzs.at[1], wzr.at[1], zs_sem.at[1], zr_sem.at[1], node_dev(z - 1))

    for tick in range(n - 1):
        kr = tick - z
        kl = tick - (n - 1 - z)

        @pl.when(kr >= 0)
        def _():
            backward_products(n - 1 - kr)
            pass_on(right_copy, kr, sr, rr, n - 1 - kr, has_left)

        @pl.when(kl >= 0)
        def _():
            backward_products(kl)
            pass_on(left_copy, kl, sl, rl, kl, has_right)

        if tick == 0:
            own = wgs[f]
            for d in range(1, nf):
                v_copy(d).wait_recv()
                own = own + wgr[d - 1]
            wz[...] = own

            @pl.when(jnp.logical_not(has_left))
            def _():
                wzs[0] = wz[...]
                z_right().start()

            @pl.when(jnp.logical_not(has_right))
            def _():
                wzs[1] = wz[...]
                z_left().start()

        if tick > 0:
            @pl.when(jnp.logical_and(z == tick, has_right))
            def _():
                z_right().wait_recv()
                wzs[0] = wz[...] + wzr[0]
                z_right().start()

            @pl.when(jnp.logical_and(n - 1 - z == tick, has_left))
            def _():
                z_left().wait_recv()
                wzs[1] = wz[...] + wzr[1]
                z_left().start()

    backward_products(z)

    for h in range(HALVES):
        pl.when(has_left)(lambda: right_copy(n - 1 - z, h).wait_recv())
        pl.when(has_right)(lambda: left_copy(z, h).wait_recv())
    pl.when(jnp.logical_not(has_right))(lambda: z_right().wait_recv())
    pl.when(jnp.logical_not(has_left))(lambda: z_left().wait_recv())

    @pl.when(jnp.logical_not(has_left))
    def _():
        rr[n - 1 - z] = jnp.zeros(rr.shape[1:], rr.dtype)
        wzr[0] = jnp.zeros(wzr.shape[1:], wzr.dtype)

    @pl.when(jnp.logical_not(has_right))
    def _():
        rl[z] = jnp.zeros(rl.shape[1:], rl.dtype)
        wzr[1] = jnp.zeros(wzr.shape[1:], wzr.dtype)

    for j in range(blocks):
        at = z * blocks + j
        total = prod[tops[0, at]] * tops[1, at].astype(jnp.float32)
        total = total + rr[n - 1 - z, j].astype(jnp.float32) + rl[z, j].astype(jnp.float32)
        gf_ref[:, j * blk:(j + 1) * blk] = total.astype(jnp.bfloat16)

    full = wz[...] + wzr[0] + wzr[1]
    wg_ref[...] = full[:feat, :classes]
    mean = jnp.sum(full[feat:feat + 1], axis=1, keepdims=True) / (n * blocks * blk)
    loss_ref[...] = jnp.broadcast_to(mean, loss_ref.shape)

    for s in range(n - 1):
        for h in range(HALVES):
            pl.when(jnp.logical_and(has_right, z - s >= 0))(lambda: x_right(s, h).wait_send())
            pl.when(jnp.logical_and(has_left, z + s < n))(lambda: x_left(s, h).wait_send())
            pl.when(n - 1 - s > z)(lambda: right_copy(s, h).wait_send())
            pl.when(s < z)(lambda: left_copy(s, h).wait_send())
    for d in range(1, nf):
        w_copy(d).wait_send()
        a_copy(d).wait_send()
        g_copy(d).wait_send()
        v_copy(d).wait_send()
    pl.when(has_right)(lambda: z_right().wait_send())
    pl.when(has_left)(lambda: z_left().wait_send())


def slot_lists(packed, blocks, n):
    count = packed.shape[1]
    down = lax.broadcasted_iota(jnp.int32, (count, count), 0)
    across = lax.broadcasted_iota(jnp.int32, (count, count), 1)

    def upright(row):
        return jnp.sum(jnp.where(down == across, row, 0), axis=1, keepdims=True)

    cols, live = lax.shift_right_logical(packed, 1), packed & 1
    key = cols * count + across[:1]
    key_up, cols_up, live_up = upright(key), upright(cols), upright(live)
    rank = jnp.sum((key_up < key).astype(jnp.int32), axis=0, keepdims=True)
    match = upright(rank) == across

    def in_order(values_up):
        return jnp.sum(jnp.where(match, values_up, 0), axis=0, keepdims=True)

    order, sorted_cols = in_order(down), in_order(cols_up)
    sorted_up = upright(sorted_cols)
    before = jnp.sum(jnp.where(down + 1 == across, sorted_up, 0), axis=0, keepdims=True)
    keep = jnp.where(across[:1] > 0, (before == sorted_cols).astype(jnp.int32), 0)
    lcol = sorted_cols % blocks
    found = jnp.concatenate([order, lcol, rank, in_order(live_up), keep, keep, keep, keep], axis=0)
    target = lax.broadcasted_iota(jnp.int32, (count, blocks * n), 1)
    upto = jnp.sum((cols_up <= target).astype(jnp.int32), axis=0, keepdims=True)
    has = jnp.max((cols_up == target).astype(jnp.int32), axis=0, keepdims=True)
    last = jnp.where(has > 0, (upto - 1) % (count // n), 0)
    ends = jnp.concatenate([last, has, has, has, has, has, has, has], axis=0)
    return found, ends


def local(features, weight, block_cols, block_live, block_tiles, labels):
    n, nf = lax.axis_size("node"), lax.axis_size("feat")
    rows, feat = features.shape
    blocks, slots, blk, _ = block_tiles.shape
    classes = weight.shape[1]
    pad_classes = 256 * pl.cdiv(classes, 256)
    row_classes = 16 * pl.cdiv(classes, 16)
    share = blocks // nf
    packed = (block_cols * 2 + block_live).reshape(1, blocks * slots)
    i32 = jnp.int32
    count = blocks * slots
    bf, f32 = jnp.bfloat16, jnp.float32
    vmem = pl.BlockSpec(memory_space=pltpu.VMEM)
    panel = (blocks, feat, blk)
    dma = pltpu.SemaphoreType.DMA
    scratch = [pltpu.VMEM(panel, bf) for _ in range(2 * n - 1)] + [
        pltpu.VMEM((blocks * slots, blk, blk), bf),
        pltpu.VMEM((blocks * slots, feat, blk), f32),
        pltpu.VMEM(panel, bf),
        pltpu.VMEM((nf, share, feat, blk), bf),
        pltpu.VMEM((nf, share, feat, blk), bf),
        pltpu.VMEM(panel, bf),
        pltpu.VMEM((nf, feat, pad_classes), bf),
        pltpu.VMEM((nf, feat + 8, pad_classes), f32),
        pltpu.VMEM((nf - 1, feat + 8, pad_classes), f32),
        pltpu.VMEM((feat + 8, pad_classes), f32),
        pltpu.VMEM((2, feat + 8, pad_classes), f32),
        pltpu.VMEM((2, feat + 8, pad_classes), f32),
        pltpu.VMEM((n - 1,) + panel, bf),
        pltpu.VMEM((n - 1,) + panel, bf),
        pltpu.VMEM((n,) + panel, bf),
        pltpu.VMEM((n,) + panel, bf),
        dma, dma((2, n - 1, HALVES)), dma((2, n - 1, HALVES)),
        dma((nf - 1,)), dma((nf - 1,)), dma((nf - 1,)), dma((nf - 1,)),
        dma((nf - 1,)), dma((nf - 1,)), dma((nf - 1,)), dma((nf - 1,)),
        dma((2,)), dma((2,)), dma((2, n, HALVES)), dma((2, n, HALVES)),
        pltpu.VMEM((8, count), i32), pltpu.VMEM((8, blocks * n), i32),
        pltpu.SMEM((8, count), i32), pltpu.SMEM((8, blocks * n), i32), dma((2,)),
    ]
    loss, weight_grad, turned = pl.pallas_call(
        functools.partial(kernel, (n, nf, classes, pad_classes, row_classes, slots)),
        out_shape=(
            jax.ShapeDtypeStruct((8, 128), f32),
            jax.ShapeDtypeStruct((feat, classes), f32),
            jax.ShapeDtypeStruct((feat, rows), bf),
        ),
        in_specs=[vmem, vmem, vmem, vmem, pl.BlockSpec(memory_space=pl.ANY)],
        out_specs=(vmem, vmem, vmem),
        scratch_shapes=scratch,
        compiler_params=pltpu.CompilerParams(
            collective_id=0, has_side_effects=True, vmem_limit_bytes=56 * 1024 * 1024),
    )(features.T, weight, labels.reshape(blocks, blk), packed,
      block_tiles.reshape(blocks * slots, blk, blk))
    return loss[0, :1], weight_grad, turned.T


def solution(mesh):
    placed = (
        P(("groups", "node"), "feat"),
        P("feat", None),
        P(("groups", "node"), None),
        P(("groups", "node"), None),
        P(("groups", "node"), None, None, None),
        P(("groups", "node")),
    )
    return jax.shard_map(
        local,
        mesh=mesh,
        in_specs=placed,
        out_specs=(P("groups"), P(("groups", "feat"), None), P(("groups", "node"), "feat")),
        check_vma=False,
    )
```

```python
import functools

import jax
import jax.numpy as jnp
from jax import lax
from jax.experimental import pallas as pl
from jax.experimental.pallas import tpu as pltpu
from jax.sharding import PartitionSpec as P

MESH = pl.DeviceIdType.MESH
NT = (((1,), (1,)), ((), ()))
UNROLL = 16
HALVES = 2


def kernel(dims, *refs):
    n, nf, classes, pad_classes, row_classes, slots = dims
    (x_ref, w_ref, lab_ref, col_ref, live_ref, tiles_hbm) = refs[:6]
    loss_ref, wg_ref, gf_ref = refs[6:9]
    rest = list(refs[9:])
    xown = rest.pop(0)
    xr = [rest.pop(0) for _ in range(n - 1)]
    xl = [rest.pop(0) for _ in range(n - 1)]
    (tiles, prod, agg, agr, gsend, gback, wfull, wgs, wgr, wz, wzs, wzr,
     sr, sl, rr, rl, tile_sem, xs_sem, xr_sem, ws_sem, wr_sem, as_sem, ar_sem,
     gs_sem, gr_sem, vs_sem, vr_sem, zs_sem, zr_sem, rs_sem, rv_sem,
     found, ends, lists, tops, list_sem) = rest

    blocks, feat, blk = xown.shape
    share = blocks // nf
    per = blocks * slots // n
    unroll = min(UNROLL, per)
    half = blocks // HALVES
    z = lax.axis_index("node")
    f = lax.axis_index("feat")
    has_right, has_left = z < n - 1, z > 0

    def node_dev(i):
        return {"node": i}

    def feat_dev(i):
        return {"feat": i}

    def send(src, dst, s_sem, r_sem, device):
        return pltpu.make_async_remote_copy(
            src_ref=src, dst_ref=dst, send_sem=s_sem, recv_sem=r_sem,
            device_id=device, device_id_type=MESH)

    tile_copy = pltpu.make_async_copy(tiles_hbm, tiles, tile_sem)
    tile_copy.start()

    barrier = pltpu.get_barrier_semaphore()
    for d in range(1, nf):
        pl.semaphore_signal(barrier, inc=1, device_id=feat_dev(lax.rem(f + d, nf)), device_id_type=MESH)

    @pl.when(has_right)
    def _():
        pl.semaphore_signal(barrier, inc=1, device_id=node_dev(z + 1), device_id_type=MESH)

    @pl.when(has_left)
    def _():
        pl.semaphore_signal(barrier, inc=1, device_id=node_dev(z - 1), device_id_type=MESH)

    for b in range(blocks):
        xown[b] = x_ref[:, b * blk:(b + 1) * blk]
    wfull[f] = jnp.concatenate(
        [w_ref[...], jnp.zeros((feat, pad_classes - classes), jnp.bfloat16)], axis=1)
    pl.semaphore_wait(barrier, nf - 1 + has_right.astype(jnp.int32) + has_left.astype(jnp.int32))

    def part(ref, h):
        return ref.at[pl.ds(h * half, half)]

    def x_right(s, h):
        return send(part(xown if s == 0 else xr[s - 1], h), part(xr[s], h),
                    xs_sem.at[0, s, h], xr_sem.at[0, s, h], node_dev(z + 1))

    def x_left(s, h):
        return send(part(xown if s == 0 else xl[s - 1], h), part(xl[s], h),
                    xs_sem.at[1, s, h], xr_sem.at[1, s, h], node_dev(z - 1))

    for h in range(HALVES):
        pl.when(has_right)(lambda: x_right(0, h).start())
        pl.when(has_left)(lambda: x_left(0, h).start())

    def w_copy(d):
        return send(wfull.at[f], wfull.at[f], ws_sem.at[d - 1], wr_sem.at[d - 1],
                    feat_dev(lax.rem(f + d, nf)))

    for d in range(1, nf):
        w_copy(d).start()

    found[...], ends[...] = slot_lists(col_ref[...] * 2 + live_ref[...], n)
    list_copy = pltpu.make_async_copy(found, lists, list_sem.at[0])
    top_copy = pltpu.make_async_copy(ends, tops, list_sem.at[1])
    list_copy.start()
    top_copy.start()
    list_copy.wait()
    top_copy.wait()

    tile_copy.wait()

    def forward_products(buf, owner):
        base = owner * per

        def body(step, carry):
            for u in range(unroll):
                t = base + step * unroll + u
                product = lax.dot_general(buf[lists[1, t]], tiles[lists[0, t]], NT,
                                       preferred_element_type=jnp.float32)
                prod[t] = product * lists[3, t].astype(jnp.float32)
            return carry

        lax.fori_loop(0, per // unroll, body, 0)

    forward_products(xown, z)
    for s in range(n - 1):
        for h in range(HALVES):
            @pl.when(z - 1 - s >= 0)
            def _():
                x_right(s, h).wait_recv()
                if s + 1 < n - 1:
                    pl.when(has_right)(lambda: x_right(s + 1, h).start())

            @pl.when(z + 1 + s < n)
            def _():
                x_left(s, h).wait_recv()
                if s + 1 < n - 1:
                    pl.when(has_left)(lambda: x_left(s + 1, h).start())

        pl.when(z - 1 - s >= 0)(lambda: forward_products(xr[s], z - 1 - s))
        pl.when(z + 1 + s < n)(lambda: forward_products(xl[s], z + 1 + s))

    def a_copy(d):
        peer = lax.rem(f + d, nf)
        return send(agg.at[pl.ds(peer * share, share)], agr.at[f], as_sem.at[d - 1], ar_sem.at[d - 1],
                    feat_dev(peer))

    def sum_rows(first):
        def body(i, carry):
            row = first + i
            total = prod[lists[2, row]]
            for s in range(1, slots):
                total = total + prod[lists[2, s * blocks + row]]
            agg[row] = total.astype(jnp.bfloat16)
            return carry

        lax.fori_loop(0, share, body, 0)

    far_first = sorted(range(1, nf), key=lambda d: abs(d - nf // 2))
    for d in far_first:
        sum_rows(lax.rem(f + d, nf) * share)
        a_copy(d).start()
    sum_rows(f * share)
    agr[f] = agg[pl.ds(f * share, share)]

    for d in range(1, nf):
        w_copy(d).wait_recv()
    w_all = jnp.concatenate([wfull[i] for i in range(nf)], axis=0)
    w_turned = w_all.astype(jnp.float32).T.astype(jnp.bfloat16)[:row_classes]
    for d in range(1, nf):
        a_copy(d).wait_recv()

    class_row = lax.broadcasted_iota(jnp.int32, (row_classes, 2 * blk), 0)
    loss_row = jnp.zeros((1, 2 * blk), jnp.float32)
    wg = None
    for b in range(0, share, 2):
        whole = jnp.concatenate(
            [jnp.concatenate([agr[i, b + c] for i in range(nf)], axis=0) for c in range(2)], axis=1)
        logits = jnp.dot(w_turned, whole, preferred_element_type=jnp.float32)
        logits = jnp.where(class_row < classes, logits, -3e38)
        label = jnp.concatenate([lab_ref[pl.ds(f * share + b + c, 1), :] for c in range(2)], axis=1)
        onehot = class_row == label
        highest = jnp.max(logits, axis=0, keepdims=True)
        grown = jnp.exp(logits - highest)
        total = jnp.sum(grown, axis=0, keepdims=True)
        picked = jnp.sum(jnp.where(onehot, logits, 0.0), axis=0, keepdims=True)
        loss_row = loss_row + (highest + jnp.log(total) - picked)
        grad = grown * (1.0 / total) - jnp.where(onehot, 1.0, 0.0)
        grad = grad.astype(jnp.bfloat16)
        grad = jnp.concatenate(
            [grad, jnp.zeros((pad_classes - row_classes, 2 * blk), jnp.bfloat16)], axis=0)
        back = jnp.dot(w_all, grad, preferred_element_type=jnp.float32).astype(jnp.bfloat16)
        for i in range(nf):
            for c in range(2):
                gsend[i, b + c] = back[i * feat:(i + 1) * feat, c * blk:(c + 1) * blk]
        more = lax.dot_general(whole, grad, NT, preferred_element_type=jnp.float32)
        wg = more if wg is None else wg + more

    def g_copy(d):
        peer = lax.rem(f + d, nf)
        return send(gsend.at[peer], gback.at[pl.ds(f * share, share)], gs_sem.at[d - 1], gr_sem.at[d - 1],
                    feat_dev(peer))

    def v_copy(d):
        peer = lax.rem(f + d, nf)
        return send(wgs.at[peer], wgr.at[d - 1], vs_sem.at[d - 1], vr_sem.at[d - 1], feat_dev(peer))

    for d in far_first:
        g_copy(d).start()
    for i in range(nf):
        wgs[i, :feat] = wg[i * feat:(i + 1) * feat]
        wgs[i, feat:] = jnp.broadcast_to(loss_row, (8, 2 * blk))
    for d in far_first:
        v_copy(d).start()
    gback[pl.ds(f * share, share)] = gsend[f]
    for d in range(1, nf):
        g_copy(d).wait_recv()

    def backward_products(owner):
        base = owner * per

        def body(step, total):
            for u in range(unroll):
                i = step * unroll + u
                t = base + i
                slot = lists[0, t]
                product = jnp.dot(gback[lax.div(slot, slots)], tiles[slot],
                               preferred_element_type=jnp.float32)
                total = product * lists[3, t].astype(jnp.float32) + total * lists[4, t].astype(jnp.float32)
                prod[i] = total
            return total

        lax.fori_loop(0, per // unroll, body, jnp.zeros((feat, blk), jnp.float32))

    def right_copy(k, h):
        return send(part(sr.at[k], h), part(rr.at[k], h), rs_sem.at[0, k, h], rv_sem.at[0, k, h], node_dev(z + 1))

    def left_copy(k, h):
        return send(part(sl.at[k], h), part(rl.at[k], h), rs_sem.at[1, k, h], rv_sem.at[1, k, h], node_dev(z - 1))

    def fill(out, came, owner, h):
        def body(j, carry):
            at = owner * blocks + j
            total = prod[tops[0, at]] * tops[1, at].astype(jnp.float32)
            if came is not None:
                total = total + came[j].astype(jnp.float32)
            out[j] = total.astype(jnp.bfloat16)
            return carry

        lax.fori_loop(h * half, (h + 1) * half, body, 0)

    def pass_on(copy, k, out, came, owner, inside):
        for h in range(HALVES):
            @pl.when(inside)
            def _():
                copy(k, h).wait_recv()
                fill(out.at[k], came.at[k], owner, h)

            pl.when(jnp.logical_not(inside))(lambda: fill(out.at[k], None, owner, h))
            copy(k, h).start()

    def z_right():
        return send(wzs.at[0], wzr.at[0], zs_sem.at[0], zr_sem.at[0], node_dev(z + 1))

    def z_left():
        return send(wzs.at[1], wzr.at[1], zs_sem.at[1], zr_sem.at[1], node_dev(z - 1))

    for tick in range(n - 1):
        kr = tick - z
        kl = tick - (n - 1 - z)

        @pl.when(kr >= 0)
        def _():
            backward_products(n - 1 - kr)
            pass_on(right_copy, kr, sr, rr, n - 1 - kr, has_left)

        @pl.when(kl >= 0)
        def _():
            backward_products(kl)
            pass_on(left_copy, kl, sl, rl, kl, has_right)

        if tick == 0:
            own = wgs[f]
            for d in range(1, nf):
                v_copy(d).wait_recv()
                own = own + wgr[d - 1]
            wz[...] = own

            @pl.when(jnp.logical_not(has_left))
            def _():
                wzs[0] = wz[...]
                z_right().start()

            @pl.when(jnp.logical_not(has_right))
            def _():
                wzs[1] = wz[...]
                z_left().start()

        if tick > 0:
            @pl.when(jnp.logical_and(z == tick, has_right))
            def _():
                z_right().wait_recv()
                wzs[0] = wz[...] + wzr[0]
                z_right().start()

            @pl.when(jnp.logical_and(n - 1 - z == tick, has_left))
            def _():
                z_left().wait_recv()
                wzs[1] = wz[...] + wzr[1]
                z_left().start()

    backward_products(z)

    for h in range(HALVES):
        pl.when(has_left)(lambda: right_copy(n - 1 - z, h).wait_recv())
        pl.when(has_right)(lambda: left_copy(z, h).wait_recv())
    pl.when(jnp.logical_not(has_right))(lambda: z_right().wait_recv())
    pl.when(jnp.logical_not(has_left))(lambda: z_left().wait_recv())

    @pl.when(jnp.logical_not(has_left))
    def _():
        rr[n - 1 - z] = jnp.zeros(rr.shape[1:], rr.dtype)
        wzr[0] = jnp.zeros(wzr.shape[1:], wzr.dtype)

    @pl.when(jnp.logical_not(has_right))
    def _():
        rl[z] = jnp.zeros(rl.shape[1:], rl.dtype)
        wzr[1] = jnp.zeros(wzr.shape[1:], wzr.dtype)

    for j in range(blocks):
        at = z * blocks + j
        total = prod[tops[0, at]] * tops[1, at].astype(jnp.float32)
        total = total + rr[n - 1 - z, j].astype(jnp.float32) + rl[z, j].astype(jnp.float32)
        gf_ref[:, j * blk:(j + 1) * blk] = total.astype(jnp.bfloat16)

    full = wz[...] + wzr[0] + wzr[1]
    wg_ref[...] = full[:feat, :classes]
    mean = jnp.sum(full[feat:feat + 1], axis=1, keepdims=True) / (n * blocks * blk)
    loss_ref[...] = jnp.broadcast_to(mean, loss_ref.shape)

    for s in range(n - 1):
        for h in range(HALVES):
            pl.when(jnp.logical_and(has_right, z - s >= 0))(lambda: x_right(s, h).wait_send())
            pl.when(jnp.logical_and(has_left, z + s < n))(lambda: x_left(s, h).wait_send())
            pl.when(n - 1 - s > z)(lambda: right_copy(s, h).wait_send())
            pl.when(s < z)(lambda: left_copy(s, h).wait_send())
    for d in range(1, nf):
        w_copy(d).wait_send()
        a_copy(d).wait_send()
        g_copy(d).wait_send()
        v_copy(d).wait_send()
    pl.when(has_right)(lambda: z_right().wait_send())
    pl.when(has_left)(lambda: z_left().wait_send())


def slot_lists(table, n):
    slots, blocks = table.shape
    count = slots * blocks
    packed = jnp.concatenate([table[s:s + 1] for s in range(slots)], axis=1)
    down = lax.broadcasted_iota(jnp.int32, (count, count), 0)
    across = lax.broadcasted_iota(jnp.int32, (count, count), 1)

    def upright(row):
        return jnp.sum(jnp.where(down == across, row, 0), axis=1, keepdims=True)

    cols, live = lax.shift_right_logical(packed, 1), packed & 1
    key = cols * count + across[:1]
    key_up, cols_up, live_up = upright(key), upright(cols), upright(live)
    rank = jnp.sum((key_up < key).astype(jnp.int32), axis=0, keepdims=True)
    match = upright(rank) == across

    def in_order(values_up):
        return jnp.sum(jnp.where(match, values_up, 0), axis=0, keepdims=True)

    order, sorted_cols = in_order(down % blocks * slots + down // blocks), in_order(cols_up)
    sorted_up = upright(sorted_cols)
    before = jnp.sum(jnp.where(down + 1 == across, sorted_up, 0), axis=0, keepdims=True)
    keep = jnp.where(across[:1] > 0, (before == sorted_cols).astype(jnp.int32), 0)
    lcol = sorted_cols % blocks
    found = jnp.concatenate([order, lcol, rank, in_order(live_up), keep, keep, keep, keep], axis=0)
    target = lax.broadcasted_iota(jnp.int32, (count, blocks * n), 1)
    upto = jnp.sum((cols_up <= target).astype(jnp.int32), axis=0, keepdims=True)
    has = jnp.max((cols_up == target).astype(jnp.int32), axis=0, keepdims=True)
    last = jnp.where(has > 0, (upto - 1) % (count // n), 0)
    ends = jnp.concatenate([last, has, has, has, has, has, has, has], axis=0)
    return found, ends


def hand_over(loss_in, wg_in, gf_in, loss_ref, wg_ref, gf_ref):
    loss_ref[0] = loss_in[0, 0]
    wg_ref[...] = wg_in[...]
    gf_ref[...] = gf_in[...]


def local(features, weight, block_cols, block_live, block_tiles, labels):
    n, nf = lax.axis_size("node"), lax.axis_size("feat")
    rows, feat = features.shape
    blocks, slots, blk, _ = block_tiles.shape
    classes = weight.shape[1]
    pad_classes = 256 * pl.cdiv(classes, 256)
    row_classes = 16 * pl.cdiv(classes, 16)
    share = blocks // nf
    i32 = jnp.int32
    count = blocks * slots
    bf, f32 = jnp.bfloat16, jnp.float32
    vmem = pl.BlockSpec(memory_space=pltpu.VMEM)
    panel = (blocks, feat, blk)
    dma = pltpu.SemaphoreType.DMA
    scratch = [pltpu.VMEM(panel, bf) for _ in range(2 * n - 1)] + [
        pltpu.VMEM((blocks * slots, blk, blk), bf),
        pltpu.VMEM((blocks * slots, feat, blk), f32),
        pltpu.VMEM(panel, bf),
        pltpu.VMEM((nf, share, feat, blk), bf),
        pltpu.VMEM((nf, share, feat, blk), bf),
        pltpu.VMEM(panel, bf),
        pltpu.VMEM((nf, feat, pad_classes), bf),
        pltpu.VMEM((nf, feat + 8, pad_classes), f32),
        pltpu.VMEM((nf - 1, feat + 8, pad_classes), f32),
        pltpu.VMEM((feat + 8, pad_classes), f32),
        pltpu.VMEM((2, feat + 8, pad_classes), f32),
        pltpu.VMEM((2, feat + 8, pad_classes), f32),
        pltpu.VMEM((n - 1,) + panel, bf),
        pltpu.VMEM((n - 1,) + panel, bf),
        pltpu.VMEM((n,) + panel, bf),
        pltpu.VMEM((n,) + panel, bf),
        dma, dma((2, n - 1, HALVES)), dma((2, n - 1, HALVES)),
        dma((nf - 1,)), dma((nf - 1,)), dma((nf - 1,)), dma((nf - 1,)),
        dma((nf - 1,)), dma((nf - 1,)), dma((nf - 1,)), dma((nf - 1,)),
        dma((2,)), dma((2,)), dma((2, n, HALVES)), dma((2, n, HALVES)),
        pltpu.VMEM((8, count), i32), pltpu.VMEM((8, blocks * n), i32),
        pltpu.SMEM((8, count), i32), pltpu.SMEM((8, blocks * n), i32), dma((2,)),
    ]
    loss, weight_grad, turned = pl.pallas_call(
        functools.partial(kernel, (n, nf, classes, pad_classes, row_classes, slots)),
        out_shape=(
            jax.ShapeDtypeStruct((8, 128), f32),
            jax.ShapeDtypeStruct((feat, classes), f32),
            jax.ShapeDtypeStruct((feat, rows), bf),
        ),
        in_specs=[vmem, vmem, vmem, vmem, vmem, pl.BlockSpec(memory_space=pl.ANY)],
        out_specs=(vmem, vmem, vmem),
        scratch_shapes=scratch,
        compiler_params=pltpu.CompilerParams(
            collective_id=0, has_side_effects=True, vmem_limit_bytes=56 * 1024 * 1024),
    )(features.T, weight, labels.reshape(blocks, blk), block_cols.T, block_live.T,
      block_tiles.reshape(blocks * slots, blk, blk))
    smem = pl.BlockSpec(memory_space=pltpu.SMEM)
    loss, weight_grad, turned = pl.pallas_call(
        hand_over,
        out_shape=(
            jax.ShapeDtypeStruct((1,), f32),
            jax.ShapeDtypeStruct((feat, classes), f32),
            jax.ShapeDtypeStruct((feat, rows), bf),
        ),
        in_specs=[smem, vmem, vmem],
        out_specs=(smem, vmem, vmem),
    )(loss, weight_grad, turned)
    return loss, weight_grad, turned.T


def solution(mesh):
    placed = (
        P(("groups", "node"), "feat"),
        P("feat", None),
        P(("groups", "node"), None),
        P(("groups", "node"), None),
        P(("groups", "node"), None, None, None),
        P(("groups", "node")),
    )
    return jax.shard_map(
        local,
        mesh=mesh,
        in_specs=placed,
        out_specs=(P("groups"), P(("groups", "feat"), None), P(("groups", "node"), "feat")),
        check_vma=False,
    )
```

```python
import functools

import jax
import jax.numpy as jnp
from jax import lax
from jax.experimental import pallas as pl
from jax.experimental.pallas import tpu as pltpu
from jax.sharding import PartitionSpec as P

MESH = pl.DeviceIdType.MESH
NT = (((1,), (1,)), ((), ()))
UNROLL = 32
HALVES = 2


def kernel(dims, *refs):
    n, nf, classes, pad_classes, row_classes, slots = dims
    (x_ref, w_ref, lab_ref, col_ref, live_ref, tiles_hbm) = refs[:6]
    loss_ref, wg_ref, gf_ref = refs[6:9]
    rest = list(refs[9:])
    xown = rest.pop(0)
    xr = [rest.pop(0) for _ in range(n - 1)]
    xl = [rest.pop(0) for _ in range(n - 1)]
    (tiles, prod, agg, agr, gsend, gback, wfull, wgs, wgr, wz, wzs, wzr,
     sr, sl, rr, rl, tile_sem, xs_sem, xr_sem, ws_sem, wr_sem, as_sem, ar_sem,
     gs_sem, gr_sem, vs_sem, vr_sem, zs_sem, zr_sem, rs_sem, rv_sem,
     found, ends, lists, tops, list_sem) = rest

    blocks, feat, blk = xown.shape
    share = blocks // nf
    per = blocks * slots // n
    unroll = min(UNROLL, per)
    half = blocks // HALVES
    z = lax.axis_index("node")
    f = lax.axis_index("feat")
    has_right, has_left = z < n - 1, z > 0

    def node_dev(i):
        return {"node": i}

    def feat_dev(i):
        return {"feat": i}

    def send(src, dst, s_sem, r_sem, device):
        return pltpu.make_async_remote_copy(
            src_ref=src, dst_ref=dst, send_sem=s_sem, recv_sem=r_sem,
            device_id=device, device_id_type=MESH)

    tile_copy = pltpu.make_async_copy(tiles_hbm, tiles, tile_sem)
    tile_copy.start()

    barrier = pltpu.get_barrier_semaphore()
    for d in range(1, nf):
        pl.semaphore_signal(barrier, inc=1, device_id=feat_dev(lax.rem(f + d, nf)), device_id_type=MESH)

    @pl.when(has_right)
    def _():
        pl.semaphore_signal(barrier, inc=1, device_id=node_dev(z + 1), device_id_type=MESH)

    @pl.when(has_left)
    def _():
        pl.semaphore_signal(barrier, inc=1, device_id=node_dev(z - 1), device_id_type=MESH)

    for b in range(blocks):
        xown[b] = x_ref[:, b * blk:(b + 1) * blk]
    wfull[f] = jnp.concatenate(
        [w_ref[...], jnp.zeros((feat, pad_classes - classes), jnp.bfloat16)], axis=1)
    pl.semaphore_wait(barrier, nf - 1 + has_right.astype(jnp.int32) + has_left.astype(jnp.int32))

    def part(ref, h):
        return ref.at[pl.ds(h * half, half)]

    def x_right(s, h):
        return send(part(xown if s == 0 else xr[s - 1], h), part(xr[s], h),
                    xs_sem.at[0, s, h], xr_sem.at[0, s, h], node_dev(z + 1))

    def x_left(s, h):
        return send(part(xown if s == 0 else xl[s - 1], h), part(xl[s], h),
                    xs_sem.at[1, s, h], xr_sem.at[1, s, h], node_dev(z - 1))

    for h in range(HALVES):
        pl.when(has_right)(lambda: x_right(0, h).start())
        pl.when(has_left)(lambda: x_left(0, h).start())

    def w_copy(d):
        return send(wfull.at[f], wfull.at[f], ws_sem.at[d - 1], wr_sem.at[d - 1],
                    feat_dev(lax.rem(f + d, nf)))

    for d in range(1, nf):
        w_copy(d).start()

    found[...], ends[...] = slot_lists(col_ref[...] * 2 + live_ref[...], n)
    list_copy = pltpu.make_async_copy(found, lists, list_sem.at[0])
    top_copy = pltpu.make_async_copy(ends, tops, list_sem.at[1])
    list_copy.start()
    top_copy.start()
    list_copy.wait()
    top_copy.wait()

    tile_copy.wait()

    def forward_products(buf, owner):
        base = owner * per

        def body(step, carry):
            for u in range(unroll):
                t = base + step * unroll + u
                product = lax.dot_general(buf[lists[1, t]], tiles[lists[0, t]], NT,
                                       preferred_element_type=jnp.float32)
                prod[t] = product * lists[3, t].astype(jnp.float32)
            return carry

        lax.fori_loop(0, per // unroll, body, 0)

    forward_products(xown, z)
    for s in range(n - 1):
        for h in range(HALVES):
            @pl.when(z - 1 - s >= 0)
            def _():
                x_right(s, h).wait_recv()
                if s + 1 < n - 1:
                    pl.when(has_right)(lambda: x_right(s + 1, h).start())

            @pl.when(z + 1 + s < n)
            def _():
                x_left(s, h).wait_recv()
                if s + 1 < n - 1:
                    pl.when(has_left)(lambda: x_left(s + 1, h).start())

        pl.when(z - 1 - s >= 0)(lambda: forward_products(xr[s], z - 1 - s))
        pl.when(z + 1 + s < n)(lambda: forward_products(xl[s], z + 1 + s))

    def a_copy(d):
        peer = lax.rem(f + d, nf)
        return send(agg.at[pl.ds(peer * share, share)], agr.at[f], as_sem.at[d - 1], ar_sem.at[d - 1],
                    feat_dev(peer))

    def sum_rows(first):
        def body(i, carry):
            row = first + i
            total = prod[lists[2, row]]
            for s in range(1, slots):
                total = total + prod[lists[2, s * blocks + row]]
            agg[row] = total.astype(jnp.bfloat16)
            return carry

        lax.fori_loop(0, share, body, 0, unroll=2)

    far_first = sorted(range(1, nf), key=lambda d: abs(d - nf // 2))
    for d in far_first:
        sum_rows(lax.rem(f + d, nf) * share)
        a_copy(d).start()
    sum_rows(f * share)
    agr[f] = agg[pl.ds(f * share, share)]

    for d in range(1, nf):
        w_copy(d).wait_recv()
    w_all = jnp.concatenate([wfull[i] for i in range(nf)], axis=0)
    w_turned = w_all.astype(jnp.float32).T.astype(jnp.bfloat16)[:row_classes]
    for d in range(1, nf):
        a_copy(d).wait_recv()

    class_row = lax.broadcasted_iota(jnp.int32, (row_classes, 2 * blk), 0)
    loss_row = jnp.zeros((1, 2 * blk), jnp.float32)
    wg = None
    for b in range(0, share, 2):
        whole = jnp.concatenate(
            [jnp.concatenate([agr[i, b + c] for i in range(nf)], axis=0) for c in range(2)], axis=1)
        logits = jnp.dot(w_turned, whole, preferred_element_type=jnp.float32)
        logits = jnp.where(class_row < classes, logits, -3e38)
        label = jnp.concatenate([lab_ref[pl.ds(f * share + b + c, 1), :] for c in range(2)], axis=1)
        onehot = class_row == label
        highest = jnp.max(logits, axis=0, keepdims=True)
        grown = jnp.exp(logits - highest)
        total = jnp.sum(grown, axis=0, keepdims=True)
        picked = jnp.sum(jnp.where(onehot, logits, 0.0), axis=0, keepdims=True)
        loss_row = loss_row + (highest + jnp.log(total) - picked)
        grad = grown * (1.0 / total) - jnp.where(onehot, 1.0, 0.0)
        grad = grad.astype(jnp.bfloat16)
        grad = jnp.concatenate(
            [grad, jnp.zeros((pad_classes - row_classes, 2 * blk), jnp.bfloat16)], axis=0)
        back = jnp.dot(w_all, grad, preferred_element_type=jnp.float32).astype(jnp.bfloat16)
        for i in range(nf):
            for c in range(2):
                gsend[i, b + c] = back[i * feat:(i + 1) * feat, c * blk:(c + 1) * blk]
        more = lax.dot_general(whole, grad, NT, preferred_element_type=jnp.float32)
        wg = more if wg is None else wg + more

    def g_copy(d):
        peer = lax.rem(f + d, nf)
        return send(gsend.at[peer], gback.at[pl.ds(f * share, share)], gs_sem.at[d - 1], gr_sem.at[d - 1],
                    feat_dev(peer))

    def v_copy(d):
        peer = lax.rem(f + d, nf)
        return send(wgs.at[peer], wgr.at[d - 1], vs_sem.at[d - 1], vr_sem.at[d - 1], feat_dev(peer))

    for d in far_first:
        g_copy(d).start()
    for i in range(nf):
        wgs[i, :feat] = wg[i * feat:(i + 1) * feat]
        wgs[i, feat:] = jnp.broadcast_to(loss_row, (8, 2 * blk))
    for d in far_first:
        v_copy(d).start()
    gback[pl.ds(f * share, share)] = gsend[f]
    for d in range(1, nf):
        g_copy(d).wait_recv()

    def backward_products(owner):
        base = owner * per

        def body(step, total):
            for u in range(unroll):
                i = step * unroll + u
                t = base + i
                slot = lists[0, t]
                product = jnp.dot(gback[lax.div(slot, slots)], tiles[slot],
                               preferred_element_type=jnp.float32)
                total = product * lists[3, t].astype(jnp.float32) + total * lists[4, t].astype(jnp.float32)
                prod[i] = total
            return total

        lax.fori_loop(0, per // unroll, body, jnp.zeros((feat, blk), jnp.float32))

    def right_copy(k, h):
        return send(part(sr.at[k], h), part(rr.at[k], h), rs_sem.at[0, k, h], rv_sem.at[0, k, h], node_dev(z + 1))

    def left_copy(k, h):
        return send(part(sl.at[k], h), part(rl.at[k], h), rs_sem.at[1, k, h], rv_sem.at[1, k, h], node_dev(z - 1))

    def fill(out, came, owner, h):
        def body(j, carry):
            at = owner * blocks + j
            total = prod[tops[0, at]] * tops[1, at].astype(jnp.float32)
            if came is not None:
                total = total + came[j].astype(jnp.float32)
            out[j] = total.astype(jnp.bfloat16)
            return carry

        lax.fori_loop(h * half, (h + 1) * half, body, 0, unroll=4)

    def pass_on(copy, k, out, came, owner, inside):
        for h in range(HALVES):
            @pl.when(inside)
            def _():
                copy(k, h).wait_recv()
                fill(out.at[k], came.at[k], owner, h)

            pl.when(jnp.logical_not(inside))(lambda: fill(out.at[k], None, owner, h))
            copy(k, h).start()

    def z_right():
        return send(wzs.at[0], wzr.at[0], zs_sem.at[0], zr_sem.at[0], node_dev(z + 1))

    def z_left():
        return send(wzs.at[1], wzr.at[1], zs_sem.at[1], zr_sem.at[1], node_dev(z - 1))

    for tick in range(n - 1):
        kr = tick - z
        kl = tick - (n - 1 - z)

        @pl.when(kr >= 0)
        def _():
            backward_products(n - 1 - kr)
            pass_on(right_copy, kr, sr, rr, n - 1 - kr, has_left)

        @pl.when(kl >= 0)
        def _():
            backward_products(kl)
            pass_on(left_copy, kl, sl, rl, kl, has_right)

        if tick == 0:
            own = wgs[f]
            for d in range(1, nf):
                v_copy(d).wait_recv()
                own = own + wgr[d - 1]
            wz[...] = own

            @pl.when(jnp.logical_not(has_left))
            def _():
                wzs[0] = wz[...]
                z_right().start()

            @pl.when(jnp.logical_not(has_right))
            def _():
                wzs[1] = wz[...]
                z_left().start()

        if tick > 0:
            @pl.when(jnp.logical_and(z == tick, has_right))
            def _():
                z_right().wait_recv()
                wzs[0] = wz[...] + wzr[0]
                z_right().start()

            @pl.when(jnp.logical_and(n - 1 - z == tick, has_left))
            def _():
                z_left().wait_recv()
                wzs[1] = wz[...] + wzr[1]
                z_left().start()

    backward_products(z)

    for h in range(HALVES):
        pl.when(has_left)(lambda: right_copy(n - 1 - z, h).wait_recv())
        pl.when(has_right)(lambda: left_copy(z, h).wait_recv())
    pl.when(jnp.logical_not(has_right))(lambda: z_right().wait_recv())
    pl.when(jnp.logical_not(has_left))(lambda: z_left().wait_recv())

    @pl.when(jnp.logical_not(has_left))
    def _():
        rr[n - 1 - z] = jnp.zeros(rr.shape[1:], rr.dtype)
        wzr[0] = jnp.zeros(wzr.shape[1:], wzr.dtype)

    @pl.when(jnp.logical_not(has_right))
    def _():
        rl[z] = jnp.zeros(rl.shape[1:], rl.dtype)
        wzr[1] = jnp.zeros(wzr.shape[1:], wzr.dtype)

    for j in range(blocks):
        at = z * blocks + j
        total = prod[tops[0, at]] * tops[1, at].astype(jnp.float32)
        total = total + rr[n - 1 - z, j].astype(jnp.float32) + rl[z, j].astype(jnp.float32)
        gf_ref[:, j * blk:(j + 1) * blk] = total.astype(jnp.bfloat16)

    full = wz[...] + wzr[0] + wzr[1]
    wg_ref[...] = full[:feat, :classes]
    mean = jnp.sum(full[feat:feat + 1], axis=1, keepdims=True) / (n * blocks * blk)
    loss_ref[...] = jnp.broadcast_to(mean, loss_ref.shape)

    for s in range(n - 1):
        for h in range(HALVES):
            pl.when(jnp.logical_and(has_right, z - s >= 0))(lambda: x_right(s, h).wait_send())
            pl.when(jnp.logical_and(has_left, z + s < n))(lambda: x_left(s, h).wait_send())
            pl.when(n - 1 - s > z)(lambda: right_copy(s, h).wait_send())
            pl.when(s < z)(lambda: left_copy(s, h).wait_send())
    for d in range(1, nf):
        w_copy(d).wait_send()
        a_copy(d).wait_send()
        g_copy(d).wait_send()
        v_copy(d).wait_send()
    pl.when(has_right)(lambda: z_right().wait_send())
    pl.when(has_left)(lambda: z_left().wait_send())


def slot_lists(table, n):
    slots, blocks = table.shape
    count = slots * blocks
    packed = jnp.concatenate([table[s:s + 1] for s in range(slots)], axis=1)
    down = lax.broadcasted_iota(jnp.int32, (count, count), 0)
    across = lax.broadcasted_iota(jnp.int32, (count, count), 1)

    def upright(row):
        return jnp.sum(jnp.where(down == across, row, 0), axis=1, keepdims=True)

    cols, live = lax.shift_right_logical(packed, 1), packed & 1
    key = cols * count + across[:1]
    key_up, cols_up, live_up = upright(key), upright(cols), upright(live)
    rank = jnp.sum((key_up < key).astype(jnp.int32), axis=0, keepdims=True)
    match = upright(rank) == across

    def in_order(values_up):
        return jnp.sum(jnp.where(match, values_up, 0), axis=0, keepdims=True)

    order, sorted_cols = in_order(down % blocks * slots + down // blocks), in_order(cols_up)
    sorted_up = upright(sorted_cols)
    before = jnp.sum(jnp.where(down + 1 == across, sorted_up, 0), axis=0, keepdims=True)
    keep = jnp.where(across[:1] > 0, (before == sorted_cols).astype(jnp.int32), 0)
    lcol = sorted_cols % blocks
    found = jnp.concatenate([order, lcol, rank, in_order(live_up), keep, keep, keep, keep], axis=0)
    target = lax.broadcasted_iota(jnp.int32, (count, blocks * n), 1)
    upto = jnp.sum((cols_up <= target).astype(jnp.int32), axis=0, keepdims=True)
    has = jnp.max((cols_up == target).astype(jnp.int32), axis=0, keepdims=True)
    last = jnp.where(has > 0, (upto - 1) % (count // n), 0)
    ends = jnp.concatenate([last, has, has, has, has, has, has, has], axis=0)
    return found, ends


def hand_over(loss_in, wg_in, gf_in, loss_ref, wg_ref, gf_ref):
    loss_ref[0] = loss_in[0, 0]
    wg_ref[...] = wg_in[...]
    gf_ref[...] = gf_in[...]


def local(features, weight, block_cols, block_live, block_tiles, labels):
    n, nf = lax.axis_size("node"), lax.axis_size("feat")
    rows, feat = features.shape
    blocks, slots, blk, _ = block_tiles.shape
    classes = weight.shape[1]
    pad_classes = 256 * pl.cdiv(classes, 256)
    row_classes = 16 * pl.cdiv(classes, 16)
    share = blocks // nf
    i32 = jnp.int32
    count = blocks * slots
    bf, f32 = jnp.bfloat16, jnp.float32
    vmem = pl.BlockSpec(memory_space=pltpu.VMEM)
    panel = (blocks, feat, blk)
    dma = pltpu.SemaphoreType.DMA
    scratch = [pltpu.VMEM(panel, bf) for _ in range(2 * n - 1)] + [
        pltpu.VMEM((blocks * slots, blk, blk), bf),
        pltpu.VMEM((blocks * slots, feat, blk), f32),
        pltpu.VMEM(panel, bf),
        pltpu.VMEM((nf, share, feat, blk), bf),
        pltpu.VMEM((nf, share, feat, blk), bf),
        pltpu.VMEM(panel, bf),
        pltpu.VMEM((nf, feat, pad_classes), bf),
        pltpu.VMEM((nf, feat + 8, pad_classes), f32),
        pltpu.VMEM((nf - 1, feat + 8, pad_classes), f32),
        pltpu.VMEM((feat + 8, pad_classes), f32),
        pltpu.VMEM((2, feat + 8, pad_classes), f32),
        pltpu.VMEM((2, feat + 8, pad_classes), f32),
        pltpu.VMEM((n - 1,) + panel, bf),
        pltpu.VMEM((n - 1,) + panel, bf),
        pltpu.VMEM((n,) + panel, bf),
        pltpu.VMEM((n,) + panel, bf),
        dma, dma((2, n - 1, HALVES)), dma((2, n - 1, HALVES)),
        dma((nf - 1,)), dma((nf - 1,)), dma((nf - 1,)), dma((nf - 1,)),
        dma((nf - 1,)), dma((nf - 1,)), dma((nf - 1,)), dma((nf - 1,)),
        dma((2,)), dma((2,)), dma((2, n, HALVES)), dma((2, n, HALVES)),
        pltpu.VMEM((8, count), i32), pltpu.VMEM((8, blocks * n), i32),
        pltpu.SMEM((8, count), i32), pltpu.SMEM((8, blocks * n), i32), dma((2,)),
    ]
    loss, weight_grad, turned = pl.pallas_call(
        functools.partial(kernel, (n, nf, classes, pad_classes, row_classes, slots)),
        out_shape=(
            jax.ShapeDtypeStruct((8, 128), f32),
            jax.ShapeDtypeStruct((feat, classes), f32),
            jax.ShapeDtypeStruct((feat, rows), bf),
        ),
        in_specs=[vmem, vmem, vmem, vmem, vmem, pl.BlockSpec(memory_space=pl.ANY)],
        out_specs=(vmem, vmem, vmem),
        scratch_shapes=scratch,
        compiler_params=pltpu.CompilerParams(
            collective_id=0, has_side_effects=True, vmem_limit_bytes=56 * 1024 * 1024),
    )(features.T, weight, labels.reshape(blocks, blk), block_cols.T, block_live.T,
      block_tiles.reshape(blocks * slots, blk, blk))
    smem = pl.BlockSpec(memory_space=pltpu.SMEM)
    loss, weight_grad, turned = pl.pallas_call(
        hand_over,
        out_shape=(
            jax.ShapeDtypeStruct((1,), f32),
            jax.ShapeDtypeStruct((feat, classes), f32),
            jax.ShapeDtypeStruct((feat, rows), bf),
        ),
        in_specs=[smem, vmem, vmem],
        out_specs=(smem, vmem, vmem),
    )(loss, weight_grad, turned)
    return loss, weight_grad, turned.T


def solution(mesh):
    placed = (
        P(("groups", "node"), "feat"),
        P("feat", None),
        P(("groups", "node"), None),
        P(("groups", "node"), None),
        P(("groups", "node"), None, None, None),
        P(("groups", "node")),
    )
    return jax.shard_map(
        local,
        mesh=mesh,
        in_specs=placed,
        out_specs=(P("groups"), P(("groups", "feat"), None), P(("groups", "node"), "feat")),
        check_vma=False,
    )
```
